32 devices in a mesh: docs: 8 (over z, y), split: 4 (over x, core).
Axes of the slice: x: 2, y: 2, z: 4, core: 2. Of those that a mesh axis runs over, the one named last changes fastest.
Arguments:
- embeddings: bfloat16 [4096, 1024], P(('docs', 'split')), may hold values from -480 to 480
- cluster_id: int32 [4096], P(('docs', 'split')), may hold values from 0 to 15, as said below
- rank: int32 [4096], P(('docs', 'split')), may hold values from 0 to 4095, each once
Outputs:
- dup_score: float32 [4096], P(('docs', 'split'))
The draws below stay inside these ranges and needn't reach their ends.
Inputs may be any that keep to these rules, and one draw needn't show every extreme that they name: `cluster_id`: cluster c belongs to owner c // 2. In each aligned block of 128 documents (the documents of one device) at most 32 documents belong to any one owner, and one owner receives exactly 32 from every block.
All inputs are finite; a program needn't handle non-finite values.
Results may differ from the reference program's by a relative error of at most 0.00056.
Values may be sent and summed in bfloat16 or wider, within the bound.
A program may use at most 64 MiB of HBM per device.

```python
import math
import jax
import jax.numpy as jnp
from jax import lax

D = 1024
DOC_DEV = 128
CL_DEV = 2
CLUSTERS = 16
NDOC = 4096
OWNER_MAX = 1024


def doc_clusters(key):
    base_key = jax.random.fold_in(key, 7)
    owners = CLUSTERS // CL_DEV
    blocks = NDOC // DOC_DEV
    base_count = DOC_DEV // owners
    key_hot, key_low, key_blocks = jax.random.split(base_key, 3)
    hot = jax.random.randint(key_hot, (), 0, owners)
    low_shift = jax.random.randint(key_low, (owners,), 0, base_count + 1)
    block_keys = jax.random.split(key_blocks, blocks)

    def one_block(block_key):
        key_order, key_shift, key_shuffle, key_within = jax.random.split(block_key, 4)
        shuffled = jax.random.permutation(key_order, owners)
        shuffled = jnp.where(shuffled == hot, shuffled[0], shuffled).at[0].set(hot)
        firsts = shuffled[0::2]
        seconds = shuffled[1::2]
        drawn = jax.random.randint(key_shift, (owners // 2,), 0, 1 << 20)
        lower = low_shift[firsts]
        shift = lower + drawn % (base_count + 1 - lower)
        shift = shift.at[0].set(base_count)
        counts = jnp.zeros((owners,), jnp.int32).at[firsts].set(base_count + shift).at[seconds].set(base_count - shift)
        ends = jnp.cumsum(counts)
        position = jnp.arange(DOC_DEV, dtype=jnp.int32)
        owner_at = jnp.searchsorted(ends, position, side='right').astype(jnp.int32)
        owner_at = jax.random.permutation(key_shuffle, owner_at)
        within = jax.random.randint(key_within, (DOC_DEV,), 0, CL_DEV)
        return owner_at * CL_DEV + within
    return jax.vmap(one_block)(block_keys).reshape(-1).astype(jnp.int32)


def draw_cluster_id(key, part):
    return doc_clusters(key)


def draw_embeddings(key, part):
    clusters = doc_clusters(key)
    topics = 48
    key_center, key_topic, key_pick, key_noise, key_scale, key_column, key_row = jax.random.split(jax.random.fold_in(key, 11), 7)
    centers = jax.random.truncated_normal(key_center, -4.0, 4.0, (CLUSTERS, D), jnp.float32)
    topic_rows = jax.random.truncated_normal(key_topic, -4.0, 4.0, (CLUSTERS * topics, D), jnp.float32)
    topic_id = clusters * topics + jax.random.randint(key_pick, (NDOC,), 0, topics)
    column_scale = jnp.exp(jax.random.uniform(key_column, (1, D), jnp.float32, math.log(0.3), math.log(3.0)))
    row_scale = jnp.exp(jax.random.uniform(key_row, (NDOC, 1), jnp.float32, 0.0, math.log(10.0)))
    noise = jax.random.truncated_normal(key_noise, -4.0, 4.0, (NDOC, D), jnp.float32)
    spread = jnp.exp(jax.random.uniform(key_scale, (NDOC, 1), jnp.float32, math.log(0.2), math.log(2.0)))
    values = (centers[clusters] + topic_rows[topic_id] + spread * noise) * column_scale * row_scale
    return values.astype(jnp.bfloat16)


def setup_inputs(seed: int = 0) -> dict:
    keys = jax.random.split(jax.random.key(seed), 4)
    embeddings = draw_embeddings(jax.random.fold_in(keys[3], 71), 0)
    cluster_id = draw_cluster_id(jax.random.fold_in(keys[3], 71), 0)
    rank = jax.random.permutation(keys[2], NDOC).astype(jnp.int32)
    return {"embeddings": embeddings, "cluster_id": cluster_id, "rank": rank}


EPSILON = 1e-06

def reference(embeddings, cluster_id, rank):
    values = embeddings.astype(jnp.float32)
    unit = (values / jnp.sqrt(lax.optimization_barrier(jnp.sum(values * values, axis=1, keepdims=True)) + EPSILON)).astype(jnp.bfloat16)
    owners = CLUSTERS // CL_DEV
    owner = (cluster_id // CL_DEV).astype(jnp.int32)
    order = jnp.argsort(owner, stable=True).astype(jnp.int32)
    counts = jax.ops.segment_sum(jnp.ones((NDOC,), jnp.int32), owner, owners).astype(jnp.int32)
    offsets = (jnp.cumsum(counts) - counts).astype(jnp.int32)
    sorted_rows = jnp.concatenate([unit[order], jnp.zeros((OWNER_MAX, D), jnp.bfloat16)], axis=0)
    sorted_cluster = jnp.concatenate([cluster_id[order], jnp.full((OWNER_MAX,), -1, jnp.int32)]).astype(jnp.int32)
    sorted_rank = jnp.concatenate([rank[order], jnp.zeros((OWNER_MAX,), jnp.int32)]).astype(jnp.int32)

    def per_owner(first_row):
        rows_here = lax.dynamic_slice_in_dim(sorted_rows, first_row, OWNER_MAX, 0)
        cluster_here = lax.dynamic_slice_in_dim(sorted_cluster, first_row, OWNER_MAX, 0)
        rank_here = lax.dynamic_slice_in_dim(sorted_rank, first_row, OWNER_MAX, 0)
        gram = jnp.dot(rows_here, rows_here.T, preferred_element_type=jnp.float32)
        allowed = (cluster_here[:, None] == cluster_here[None, :]) & (rank_here[None, :] < rank_here[:, None])
        return lax.optimization_barrier(jnp.max(jnp.where(allowed, gram, -1.0), axis=1))
    top_scores = lax.map(per_owner, offsets)
    sorted_owner = owner[order]
    within = (jnp.arange(NDOC).astype(jnp.int32) - offsets[sorted_owner]).astype(jnp.int32)
    picked = top_scores[sorted_owner, within]
    return jnp.zeros((NDOC,), jnp.float32).at[order].set(picked)
```

```python
import functools

import jax
import jax.numpy as jnp
from jax import lax
from jax.experimental import pallas as pl
from jax.experimental.pallas import tpu as pltpu
from jax.sharding import PartitionSpec as P

CL_DEV = 2
EPSILON = 1e-06
LANES = 128
ROW_TILE = 16
UNROLL_UP_TO = 8
MESH = pl.DeviceIdType.MESH


def xor(a, b, size):
    out, bit = 0, 1
    while bit < size:
        out = out + bit * (((a // bit) + (b // bit)) % 2)
        bit *= 2
    return out


def each(start, stop, body):
    if stop - start <= UNROLL_UP_TO:
        for i in range(start, stop):
            body(i)
    else:
        lax.fori_loop(start, stop, lambda i, c: (body(i), c)[1], 0)


def kernel(
    owners, peers, cap, total,
    emb_ref, cluster_ref, rank_ref, out_ref,
    send_rows, rows, send_keys, got_keys, key_rows, key_cols, scores, got_scores,
    rows_out, rows_in, fwd_out, fwd_in, keys_out, keys_in, kfwd_out, kfwd_in, back_out, back_in,
):
    docs, width = emb_ref.shape
    per = LANES // cap
    groups = key_rows.shape[1]
    me = lax.axis_index("docs")
    mine = lax.axis_index("split")

    def across(k):
        return {"docs": xor(me, k, owners)}

    def beside(j):
        return {"split": xor(mine, j, peers)}

    barrier = pltpu.get_barrier_semaphore()
    each(1, owners, lambda k: pl.semaphore_signal(barrier, inc=1, device_id=across(k), device_id_type=MESH))
    for j in range(1, peers):
        pl.semaphore_signal(barrier, inc=1, device_id=beside(j), device_id_type=MESH)

    def copy(src, dst, out_sem, in_sem, device):
        return pltpu.make_async_remote_copy(
            src_ref=src, dst_ref=dst, send_sem=out_sem, recv_sem=in_sem, device_id=device, device_id_type=MESH
        )

    def rows_copy(k):
        return copy(send_rows.at[k], rows.at[0, k], rows_out.at[k], rows_in.at[k], across(k))

    def forward_copy(j, bit, k):
        return copy(rows.at[j, k], rows.at[j + bit, k], fwd_out.at[j + bit, k], fwd_in.at[j + bit, k], beside(bit))

    def key_copy(k):
        return copy(send_keys.at[k], got_keys.at[k], keys_out.at[k], keys_in.at[k], across(k))

    def key_forward(j):
        return copy(key_rows.at[0], key_rows.at[j], kfwd_out.at[j], kfwd_in.at[j], beside(j))

    def back_copy(k):
        return copy(scores.at[k // per], got_scores.at[k], back_out.at[k], back_in.at[k], across(k))

    row_id = lax.broadcasted_iota(jnp.int32, (docs, docs), 0)
    lane_id = lax.broadcasted_iota(jnp.int32, (docs, docs), 1)
    eye = row_id == lane_id

    def column(row):
        return jnp.sum(jnp.where(eye, row, 0.0), axis=1, keepdims=True)

    cluster = cluster_ref[...]
    owner = lax.shift_right_logical(cluster, CL_DEV.bit_length() - 1)
    local = cluster - owner * CL_DEV
    key = (local + 1).astype(jnp.float32) * total + rank_ref[...].astype(jnp.float32)
    rel = jnp.bitwise_xor(owner, me).astype(jnp.float32)
    rel_col, key_col = column(rel), column(key)
    same = rel_col == rel
    before = jnp.sum(jnp.where(same & (row_id < lane_id), 1.0, 0.0), axis=0, keepdims=True)
    before_col = jnp.sum(jnp.where(same & (lane_id < row_id), 1.0, 0.0), axis=1, keepdims=True)
    target = (rel * cap + before).astype(jnp.int32)
    lanes = lax.broadcasted_iota(jnp.int32, (docs, LANES), 1)
    slot_col = before_col.astype(jnp.int32)

    def make_keys(k):
        here = (rel_col == jnp.float32(k) if isinstance(k, int) else rel_col == k.astype(jnp.float32))
        return jnp.sum(
            jnp.where(here & (lanes == slot_col + (k % per) * cap), key_col, 0.0), axis=0, keepdims=True
        )

    def put_keys(k):
        send_keys[k] = make_keys(k)

    each(1, owners, put_keys)
    got_keys[0] = make_keys(0)

    values = emb_ref[...].astype(jnp.float32)
    norm = jnp.sqrt(jnp.sum(values * values, axis=1, keepdims=True) + EPSILON)
    unit = (values * (1.0 / norm)).astype(jnp.bfloat16)
    slot_id = lax.broadcasted_iota(jnp.int32, (cap, docs), 0)

    def pack(k):
        pick = jnp.where(slot_id + k * cap == target, 1.0, 0.0).astype(jnp.bfloat16)
        return jnp.dot(pick, unit, preferred_element_type=jnp.float32).astype(jnp.bfloat16)

    pl.semaphore_wait(barrier, owners - 1 + peers - 1)

    each(1, owners, lambda k: key_copy(k).start())

    def send(i):
        k = owners - i
        send_rows[k] = pack(k)
        rows_copy(k).start()

    each(1, owners, send)
    rows[0, 0] = pack(0)

    bits = []
    bit = peers // 2
    while bit:
        bits.append(bit)
        bit //= 2

    def held(level):
        out = [0]
        for b in bits[:level]:
            out = out + [j + b for j in out]
        return out

    def forward(level_from, j, k):
        for b in bits[level_from:]:
            forward_copy(j, b, k).start()

    def level_of(j):
        return max((n + 1 for n, b in enumerate(bits) if j & b), default=0)

    others = sorted(range(1, peers), key=lambda j: (level_of(j), j))

    forward(0, 0, 0)

    each(1, owners, lambda k: key_copy(k).wait_recv())

    def sum_keys(g):
        if isinstance(g, int):
            acc = got_keys[g * per]
            for i in range(1, min(per, owners)):
                acc = acc + got_keys[g * per + i]
        else:
            acc = lax.fori_loop(1, per, lambda i, a: a + got_keys[g * per + i], got_keys[g * per])
        key_rows[0, g] = acc

    each(0, groups, sum_keys)
    for j in range(1, peers):
        key_forward(j).start()

    square = lax.broadcasted_iota(jnp.int32, (LANES, LANES), 0) == lax.broadcasted_iota(jnp.int32, (LANES, LANES), 1)

    def make_cols(j):
        def one(g):
            key_cols[j, g] = jnp.sum(jnp.where(square, key_rows[j, g], 0.0), axis=1, keepdims=True)

        each(0, groups, one)

    make_cols(0)

    def take(i):
        k = owners - i
        rows_copy(k).wait_recv()
        forward(0, 0, k)

    each(1, owners, take)
    for j in range(1, peers):
        key_forward(j).wait_recv()
        make_cols(j)

    size = min(2, groups)
    tile = size * LANES
    tiles = groups // size
    blocks = tile // cap

    def tile_rows(j, t):
        return rows[j, pl.ds(t * blocks, blocks)].reshape(tile, width)

    def score_chunk(j):
        def queries(qt):
            q = jnp.concatenate([key_rows[0, qt * size + i] for i in range(size)], axis=1)
            base = jnp.floor(q * (1.0 / total)) * total
            q_rows = tile_rows(0, qt)

            def keys(kt):
                c = jnp.concatenate([key_cols[j, kt * size + i] for i in range(size)], axis=0)
                dots = lax.dot_general(
                    tile_rows(j, kt), q_rows, (((1,), (1,)), ((), ())), preferred_element_type=jnp.float32
                )
                best = jnp.max(jnp.where((c < q) & (c >= base), dots, -1.0), axis=0, keepdims=True)
                for i in range(size):
                    part = best[:, i * LANES:(i + 1) * LANES]
                    scores[qt * size + i] = jnp.maximum(scores[qt * size + i], part)

            each(0, tiles, keys)

        each(0, tiles, queries)

    def clear(g):
        scores[g] = jnp.full((1, LANES), -1.0, jnp.float32)

    each(0, groups, clear)
    score_chunk(0)
    for j in others:
        b = bits[level_of(j) - 1]

        def arrive(i, j=j, b=b):
            k = owners - i if not isinstance(i, int) or i < owners else 0
            forward_copy(j - b, b, k).wait_recv()
            forward(level_of(j), j, k)

        arrive(owners)
        each(1, owners, arrive)
        if level_of(j) == len(bits):
            continue
    for j in others:
        score_chunk(j)

    each(1, owners, lambda k: back_copy(k).start())
    got_scores[0] = scores[0]
    lane_col = slot_col + ((rel_col.astype(jnp.int32) % per) * cap)
    each(1, owners, lambda k: back_copy(k).wait_recv())

    def pick(k, acc):
        kf = jnp.float32(k) if isinstance(k, int) else k.astype(jnp.float32)
        return jnp.where(rel_col == kf, got_scores[k], acc)

    found = jnp.zeros((docs, LANES), jnp.float32)
    if owners <= UNROLL_UP_TO:
        for k in range(owners):
            found = pick(k, found)
    else:
        found = lax.fori_loop(0, owners, pick, found)
    result = jnp.sum(jnp.where(lanes == lane_col, found, 0.0), axis=1, keepdims=True)
    out_ref[...] = jnp.sum(jnp.where(eye, result, 0.0), axis=0, keepdims=True)

    each(1, owners, lambda k: key_copy(k).wait_send())
    each(1, owners, lambda k: rows_copy(k).wait_send())
    each(1, owners, lambda k: back_copy(k).wait_send())
    for j in range(1, peers):
        key_forward(j).wait_send()
        b = bits[level_of(j) - 1]
        each(0, owners, lambda k, j=j, b=b: forward_copy(j - b, b, k).wait_send())


def per_device(total, embeddings, cluster_id, rank):
    owners = lax.axis_size("docs")
    peers = lax.axis_size("split")
    docs, width = embeddings.shape
    cap = 2 * docs // owners
    cap = -(-cap // ROW_TILE) * ROW_TILE
    groups = owners * cap // LANES
    dma = pltpu.SemaphoreType.DMA
    vmem = pl.BlockSpec(memory_space=pltpu.VMEM)
    out = pl.pallas_call(
        functools.partial(kernel, owners, peers, cap, float(total)),
        out_shape=jax.ShapeDtypeStruct((1, docs), jnp.float32),
        in_specs=[vmem] * 3,
        out_specs=vmem,
        scratch_shapes=[
            pltpu.VMEM((owners, cap, width), jnp.bfloat16),
            pltpu.VMEM((peers, owners, cap, width), jnp.bfloat16),
            pltpu.VMEM((owners, 1, LANES), jnp.float32),
            pltpu.VMEM((owners, 1, LANES), jnp.float32),
            pltpu.VMEM((peers, groups, 1, LANES), jnp.float32),
            pltpu.VMEM((peers, groups, LANES, 1), jnp.float32),
            pltpu.VMEM((groups, 1, LANES), jnp.float32),
            pltpu.VMEM((owners, 1, LANES), jnp.float32),
            dma((owners,)), dma((owners,)),
            dma((peers, owners)), dma((peers, owners)),
            dma((owners,)), dma((owners,)),
            dma((peers,)), dma((peers,)),
            dma((owners,)), dma((owners,)),
        ],
        compiler_params=pltpu.CompilerParams(
            collective_id=0, has_side_effects=True, vmem_limit_bytes=44 * 1024 * 1024
        ),
    )(embeddings, cluster_id.reshape(1, docs), rank.reshape(1, docs))
    return out.reshape(docs)


def solution(mesh):
    placed = (P(("docs", "split"), None), P(("docs", "split")), P(("docs", "split")))

    def run(embeddings, cluster_id, rank):
        return jax.shard_map(
            functools.partial(per_device, embeddings.shape[0]),
            mesh=mesh, in_specs=placed, out_specs=P(("docs", "split")), check_vma=False,
        )(embeddings, cluster_id, rank)

    return run
```

```python
import functools

import jax
import jax.numpy as jnp
from jax import lax
from jax.experimental import pallas as pl
from jax.experimental.pallas import tpu as pltpu
from jax.sharding import PartitionSpec as P

CL_DEV = 2
EPSILON = 1e-06
LANES = 128
ROW_TILE = 16
UNROLL_UP_TO = 8
LAG = 2
MESH = pl.DeviceIdType.MESH


def xor(a, b, size):
    out, bit = 0, 1
    while bit < size:
        out = out + bit * (((a // bit) + (b // bit)) % 2)
        bit *= 2
    return out


def each(start, stop, body):
    if stop - start <= UNROLL_UP_TO:
        for i in range(start, stop):
            body(i)
    else:
        lax.fori_loop(start, stop, lambda i, c: (body(i), c)[1], 0)


def kernel(
    owners, peers, cap, total,
    emb_hbm, cluster_hbm, rank_hbm, out_ref,
    emb_ref, cluster_ref, rank_ref, load_sems, send_rows, rows, send_keys, got_keys, key_rows, key_cols, scores, got_scores,
    rows_out, rows_in, fwd_out, fwd_in, keys_out, keys_in, kfwd_out, kfwd_in, back_out, back_in,
):
    docs, width = emb_ref.shape
    per = LANES // cap
    groups = key_rows.shape[1]
    me = lax.axis_index("docs")
    mine = lax.axis_index("split")

    def across(k):
        return {"docs": xor(me, k, owners)}

    def beside(j):
        return {"split": xor(mine, j, peers)}

    loads = [
        pltpu.make_async_copy(src, dst, load_sems.at[i])
        for i, (src, dst) in enumerate(((cluster_hbm, cluster_ref), (rank_hbm, rank_ref), (emb_hbm, emb_ref)))
    ]
    for load in loads:
        load.start()
    barrier = pltpu.get_barrier_semaphore()
    each(1, owners, lambda k: pl.semaphore_signal(barrier, inc=1, device_id=across(k), device_id_type=MESH))
    for j in range(1, peers):
        pl.semaphore_signal(barrier, inc=1, device_id=beside(j), device_id_type=MESH)

    def copy(src, dst, out_sem, in_sem, device):
        return pltpu.make_async_remote_copy(
            src_ref=src, dst_ref=dst, send_sem=out_sem, recv_sem=in_sem, device_id=device, device_id_type=MESH
        )

    def rows_copy(k):
        return copy(send_rows.at[k], rows.at[0, k], rows_out.at[k], rows_in.at[k], across(k))

    def forward_copy(j, bit, k):
        return copy(rows.at[j, k], rows.at[j + bit, k], fwd_out.at[j + bit, k], fwd_in.at[j + bit, k], beside(bit))

    def key_copy(k):
        return copy(send_keys.at[k], got_keys.at[k], keys_out.at[k], keys_in.at[k], across(k))

    def key_forward(j):
        return copy(key_rows.at[0], key_rows.at[j], kfwd_out.at[j], kfwd_in.at[j], beside(j))

    def back_copy(k):
        return copy(scores.at[k // per], got_scores.at[k], back_out.at[k], back_in.at[k], across(k))

    row_id = lax.broadcasted_iota(jnp.int32, (docs, docs), 0)
    lane_id = lax.broadcasted_iota(jnp.int32, (docs, docs), 1)
    eye = row_id == lane_id

    def column(row):
        return jnp.sum(jnp.where(eye, row, 0.0), axis=1, keepdims=True)

    loads[0].wait()
    loads[1].wait()
    cluster = cluster_ref[...]
    owner = lax.shift_right_logical(cluster, CL_DEV.bit_length() - 1)
    local = cluster - owner * CL_DEV
    key = (local + 1).astype(jnp.float32) * total + rank_ref[...].astype(jnp.float32)
    rel = jnp.bitwise_xor(owner, me).astype(jnp.float32)
    rel_col, key_col = column(rel), column(key)
    same = rel_col == rel
    before = jnp.sum(jnp.where(same & (row_id < lane_id), 1.0, 0.0), axis=0, keepdims=True)
    before_col = jnp.sum(jnp.where(same & (lane_id < row_id), 1.0, 0.0), axis=1, keepdims=True)
    target = (rel * cap + before).astype(jnp.int32)
    lanes = lax.broadcasted_iota(jnp.int32, (docs, LANES), 1)
    slot_col = before_col.astype(jnp.int32)

    def make_keys(k):
        here = (rel_col == jnp.float32(k) if isinstance(k, int) else rel_col == k.astype(jnp.float32))
        return jnp.sum(
            jnp.where(here & (lanes == slot_col + (k % per) * cap), key_col, 0.0), axis=0, keepdims=True
        )

    def put_keys(k):
        send_keys[k] = make_keys(k)

    each(1, owners, put_keys)
    got_keys[0] = make_keys(0)

    loads[2].wait()
    values = emb_ref[...].astype(jnp.float32)
    norm = jnp.sqrt(jnp.sum(values * values, axis=1, keepdims=True) + EPSILON)
    unit = (values * (1.0 / norm)).astype(jnp.bfloat16)
    slot_id = lax.broadcasted_iota(jnp.int32, (cap, docs), 0)

    def pack(k):
        pick = jnp.where(slot_id + k * cap == target, 1.0, 0.0).astype(jnp.bfloat16)
        return jnp.dot(pick, unit, preferred_element_type=jnp.float32).astype(jnp.bfloat16)

    pl.semaphore_wait(barrier, owners - 1 + peers - 1)

    each(1, owners, lambda k: key_copy(k).start())

    def send(k):
        send_rows[k] = pack(k)
        rows_copy(k).start()

    unrolled = owners <= UNROLL_UP_TO
    order = [owners - 1]
    for i in range(1, owners // 2):
        order += [i, owners - 1 - i]
    if unrolled:
        for k in order:
            send(k)
    else:
        each(1, owners, lambda i: send(owners - i))
    rows[0, 0] = pack(0)

    bits = []
    bit = peers // 2
    while bit:
        bits.append(bit)
        bit //= 2

    def held(level):
        out = [0]
        for b in bits[:level]:
            out = out + [j + b for j in out]
        return out

    def forward(level_from, j, k):
        for b in bits[level_from:]:
            forward_copy(j, b, k).start()

    def level_of(j):
        return max((n + 1 for n, b in enumerate(bits) if j & b), default=0)

    others = sorted(range(1, peers), key=lambda j: (level_of(j), j))

    forward(0, 0, 0)

    each(1, owners, lambda k: key_copy(k).wait_recv())

    def sum_keys(g):
        if isinstance(g, int):
            acc = got_keys[g * per]
            for i in range(1, min(per, owners)):
                acc = acc + got_keys[g * per + i]
        else:
            acc = lax.fori_loop(1, per, lambda i, a: a + got_keys[g * per + i], got_keys[g * per])
        key_rows[0, g] = acc

    each(0, groups, sum_keys)
    for j in range(1, peers):
        key_forward(j).start()

    square = lax.broadcasted_iota(jnp.int32, (LANES, LANES), 0) == lax.broadcasted_iota(jnp.int32, (LANES, LANES), 1)

    def make_cols(j):
        def one(g):
            key_cols[j, g] = jnp.sum(jnp.where(square, key_rows[j, g], 0.0), axis=1, keepdims=True)

        each(0, groups, one)

    make_cols(0)

    size = min(2, groups)
    tile = size * LANES
    tiles = groups // size
    blocks = tile // cap

    def tile_rows(j, t):
        return rows[j, pl.ds(t * blocks, blocks)].reshape(tile, width)

    def score_chunk(j):
        def queries(qt):
            q = jnp.concatenate([key_rows[0, qt * size + i] for i in range(size)], axis=1)
            base = jnp.floor(q * (1.0 / total)) * total
            q_rows = tile_rows(0, qt)

            def keys(kt):
                c = jnp.concatenate([key_cols[j, kt * size + i] for i in range(size)], axis=0)
                dots = lax.dot_general(
                    tile_rows(j, kt), q_rows, (((1,), (1,)), ((), ())), preferred_element_type=jnp.float32
                )
                best = jnp.max(jnp.where((c < q) & (c >= base), dots, -1.0), axis=0, keepdims=True)
                for i in range(size):
                    part = best[:, i * LANES:(i + 1) * LANES]
                    scores[qt * size + i] = jnp.maximum(scores[qt * size + i], part)

            each(0, tiles, keys)

        each(0, tiles, queries)

    def clear(g):
        scores[g] = jnp.full((1, LANES), -1.0, jnp.float32)

    each(0, groups, clear)

    def arrive(j, k):
        if j:
            b = bits[level_of(j) - 1]
            forward_copy(j - b, b, k).wait_recv()
        else:
            rows_copy(k).wait_recv()
        forward(level_of(j), j, k)

    def arrivals(level, k):
        for j in range(peers):
            if level_of(j) == level:
                arrive(j, k)

    levels = len(bits)

    def get_key_cols():
        for j in range(1, peers):
            key_forward(j).wait_recv()
            make_cols(j)

    if unrolled:
        queue = [0] + order
        for i in range(owners + LAG * (levels - 1)):
            for level in range(levels):
                if 0 <= i - LAG * level < owners and not (level == 0 and i == 0):
                    arrivals(level, queue[i - LAG * level])
            if i == owners // 2:
                get_key_cols()
            if i == owners - 1:
                score_chunk(0)
    else:
        get_key_cols()
        for level in range(1, levels):
            arrivals(level, 0)

        def step(i):
            for level in range(levels):
                arrivals(level, owners - i)

        each(1, owners, step)
        score_chunk(0)
    for j in others:
        if level_of(j) == levels:
            each(0, owners, lambda k, j=j: arrive(j, k))
        score_chunk(j)

    each(1, owners, lambda k: back_copy(k).start())
    got_scores[0] = scores[0]
    lane_col = slot_col + ((rel_col.astype(jnp.int32) % per) * cap)
    each(1, owners, lambda k: back_copy(k).wait_recv())

    def pick(k, acc):
        kf = jnp.float32(k) if isinstance(k, int) else k.astype(jnp.float32)
        return jnp.where(rel_col == kf, got_scores[k], acc)

    found = jnp.zeros((docs, LANES), jnp.float32)
    if owners <= UNROLL_UP_TO:
        for k in range(owners):
            found = pick(k, found)
    else:
        found = lax.fori_loop(0, owners, pick, found)
    result = jnp.sum(jnp.where(lanes == lane_col, found, 0.0), axis=1, keepdims=True)
    out_ref[...] = jnp.sum(jnp.where(eye, result, 0.0), axis=0, keepdims=True)

    each(1, owners, lambda k: key_copy(k).wait_send())
    each(1, owners, lambda k: rows_copy(k).wait_send())
    each(1, owners, lambda k: back_copy(k).wait_send())
    for j in range(1, peers):
        key_forward(j).wait_send()
        b = bits[level_of(j) - 1]
        each(0, owners, lambda k, j=j, b=b: forward_copy(j - b, b, k).wait_send())


def per_device(total, embeddings, cluster_id, rank):
    owners = lax.axis_size("docs")
    peers = lax.axis_size("split")
    docs, width = embeddings.shape
    cap = 2 * docs // owners
    cap = -(-cap // ROW_TILE) * ROW_TILE
    groups = owners * cap // LANES
    dma = pltpu.SemaphoreType.DMA
    vmem = pl.BlockSpec(memory_space=pltpu.VMEM)
    out = pl.pallas_call(
        functools.partial(kernel, owners, peers, cap, float(total)),
        out_shape=jax.ShapeDtypeStruct((1, docs), jnp.float32),
        in_specs=[pl.BlockSpec(memory_space=pltpu.HBM)] * 3,
        out_specs=vmem,
        scratch_shapes=[
            pltpu.VMEM((docs, width), embeddings.dtype),
            pltpu.VMEM((1, docs), jnp.int32),
            pltpu.VMEM((1, docs), jnp.int32),
            dma((3,)),
            pltpu.VMEM((owners, cap, width), jnp.bfloat16),
            pltpu.VMEM((peers, owners, cap, width), jnp.bfloat16),
            pltpu.VMEM((owners, 1, LANES), jnp.float32),
            pltpu.VMEM((owners, 1, LANES), jnp.float32),
            pltpu.VMEM((peers, groups, 1, LANES), jnp.float32),
            pltpu.VMEM((peers, groups, LANES, 1), jnp.float32),
            pltpu.VMEM((groups, 1, LANES), jnp.float32),
            pltpu.VMEM((owners, 1, LANES), jnp.float32),
            dma((owners,)), dma((owners,)),
            dma((peers, owners)), dma((peers, owners)),
            dma((owners,)), dma((owners,)),
            dma((peers,)), dma((peers,)),
            dma((owners,)), dma((owners,)),
        ],
        compiler_params=pltpu.CompilerParams(
            collective_id=0, has_side_effects=True, vmem_limit_bytes=127 * 512 * 1024
        ),
    )(embeddings, cluster_id.reshape(1, docs), rank.reshape(1, docs))
    return out.reshape(docs)


def solution(mesh):
    placed = (P(("docs", "split"), None), P(("docs", "split")), P(("docs", "split")))

    def run(embeddings, cluster_id, rank):
        return jax.shard_map(
            functools.partial(per_device, embeddings.shape[0]),
            mesh=mesh, in_specs=placed, out_specs=P(("docs", "split")), check_vma=False,
        )(embeddings, cluster_id, rank)

    return run
```

```python
import functools

import jax
import jax.numpy as jnp
from jax import lax
from jax.experimental import pallas as pl
from jax.experimental.pallas import tpu as pltpu
from jax.sharding import PartitionSpec as P

CL_DEV = 2
EPSILON = 1e-06
LANES = 128
ROW_TILE = 16
UNROLL_UP_TO = 8
LAG = 2
WINDOW = 2
MESH = pl.DeviceIdType.MESH


def xor(a, b, size):
    out, bit = 0, 1
    while bit < size:
        out = out + bit * (((a // bit) + (b // bit)) % 2)
        bit *= 2
    return out


def each(start, stop, body):
    if stop - start <= UNROLL_UP_TO:
        for i in range(start, stop):
            body(i)
    else:
        lax.fori_loop(start, stop, lambda i, c: (body(i), c)[1], 0)


def kernel(
    owners, peers, cap, total,
    emb_hbm, cluster_hbm, rank_hbm, out_ref,
    emb_ref, cluster_ref, rank_ref, load_sems, send_rows, raw_rows, rows, send_keys, got_keys, key_rows, key_cols, scores, got_scores,
    rows_out, rows_in, fwd_out, fwd_in, keys_out, keys_in, kfwd_out, kfwd_in, back_out, back_in,
):
    docs, width = emb_ref.shape
    per = LANES // cap
    groups = key_rows.shape[1]
    me = lax.axis_index("docs")
    mine = lax.axis_index("split")

    def across(k):
        return {"docs": xor(me, k, owners)}

    def beside(j):
        return {"split": xor(mine, j, peers)}

    loads = [
        pltpu.make_async_copy(src, dst, load_sems.at[i])
        for i, (src, dst) in enumerate(((cluster_hbm, cluster_ref), (rank_hbm, rank_ref), (emb_hbm, emb_ref)))
    ]
    for load in loads:
        load.start()
    barrier = pltpu.get_barrier_semaphore()
    each(1, owners, lambda k: pl.semaphore_signal(barrier, inc=1, device_id=across(k), device_id_type=MESH))
    for j in range(1, peers):
        pl.semaphore_signal(barrier, inc=1, device_id=beside(j), device_id_type=MESH)

    def copy(src, dst, out_sem, in_sem, device):
        return pltpu.make_async_remote_copy(
            src_ref=src, dst_ref=dst, send_sem=out_sem, recv_sem=in_sem, device_id=device, device_id_type=MESH
        )

    def rows_copy(k):
        return copy(send_rows.at[k], raw_rows.at[k], rows_out.at[k], rows_in.at[k], across(k))

    def forward_copy(j, bit, k):
        return copy(rows.at[j, k], rows.at[j + bit, k], fwd_out.at[j + bit, k], fwd_in.at[j + bit, k], beside(bit))

    def key_copy(k):
        return copy(send_keys.at[k], got_keys.at[k], keys_out.at[k], keys_in.at[k], across(k))

    def key_forward(j):
        return copy(key_rows.at[0], key_rows.at[j], kfwd_out.at[j], kfwd_in.at[j], beside(j))

    def back_copy(k):
        return copy(scores.at[k // per], got_scores.at[k], back_out.at[k], back_in.at[k], across(k))

    row_id = lax.broadcasted_iota(jnp.int32, (docs, docs), 0)
    lane_id = lax.broadcasted_iota(jnp.int32, (docs, docs), 1)
    eye = row_id == lane_id

    def column(row):
        return jnp.sum(jnp.where(eye, row, 0.0), axis=1, keepdims=True)

    loads[0].wait()
    loads[1].wait()
    cluster = cluster_ref[...]
    owner = lax.shift_right_logical(cluster, CL_DEV.bit_length() - 1)
    local = cluster - owner * CL_DEV
    key = (local + 1).astype(jnp.float32) * total + rank_ref[...].astype(jnp.float32)
    rel = jnp.bitwise_xor(owner, me).astype(jnp.float32)
    rel_col, key_col = column(rel), column(key)
    same = rel_col == rel
    before = jnp.sum(jnp.where(same & (row_id < lane_id), 1.0, 0.0), axis=0, keepdims=True)
    before_col = jnp.sum(jnp.where(same & (lane_id < row_id), 1.0, 0.0), axis=1, keepdims=True)
    target = (rel * cap + before).astype(jnp.int32)
    lanes = lax.broadcasted_iota(jnp.int32, (docs, LANES), 1)
    slot_col = before_col.astype(jnp.int32)

    def make_keys(k):
        here = (rel_col == jnp.float32(k) if isinstance(k, int) else rel_col == k.astype(jnp.float32))
        return jnp.sum(
            jnp.where(here & (lanes == slot_col + (k % per) * cap), key_col, 0.0), axis=0, keepdims=True
        )

    def put_keys(k):
        send_keys[k] = make_keys(k)

    each(1, owners, put_keys)
    got_keys[0] = make_keys(0)

    def unit(block):
        values = block.astype(jnp.float32)
        norm = jnp.sqrt(jnp.sum(values * values, axis=1, keepdims=True) + EPSILON)
        return (values * (1.0 / norm)).astype(jnp.bfloat16)

    loads[2].wait()
    slot_id = lax.broadcasted_iota(jnp.int32, (cap, docs), 0)

    def pack(k):
        pick = jnp.where(slot_id + k * cap == target, 1.0, 0.0).astype(jnp.bfloat16)
        return jnp.dot(pick, emb_ref[...], preferred_element_type=jnp.float32).astype(send_rows.dtype)

    pl.semaphore_wait(barrier, owners - 1 + peers - 1)

    each(1, owners, lambda k: key_copy(k).start())

    def send(k):
        send_rows[k] = pack(k)
        rows_copy(k).start()

    unrolled = owners <= UNROLL_UP_TO
    near = list(range(1, owners // 2))
    far = list(range(owners - 1, owners // 2 - 1, -1))
    if unrolled:
        for k in far[:1] + near[:1] + far[1:WINDOW] + near[1:]:
            send(k)
        for k in far[WINDOW:]:
            send_rows[k] = pack(k)
    else:
        each(1, owners, lambda i: send(owners - i))
    rows[0, 0] = unit(pack(0))

    bits = []
    bit = peers // 2
    while bit:
        bits.append(bit)
        bit //= 2

    def held(level):
        out = [0]
        for b in bits[:level]:
            out = out + [j + b for j in out]
        return out

    def forward(level_from, j, k):
        for b in bits[level_from:]:
            forward_copy(j, b, k).start()

    def level_of(j):
        return max((n + 1 for n, b in enumerate(bits) if j & b), default=0)

    others = sorted(range(1, peers), key=lambda j: (level_of(j), j))

    forward(0, 0, 0)

    each(1, owners, lambda k: key_copy(k).wait_recv())

    def sum_keys(g):
        if isinstance(g, int):
            acc = got_keys[g * per]
            for i in range(1, min(per, owners)):
                acc = acc + got_keys[g * per + i]
        else:
            acc = lax.fori_loop(1, per, lambda i, a: a + got_keys[g * per + i], got_keys[g * per])
        key_rows[0, g] = acc

    each(0, groups, sum_keys)
    for j in range(1, peers):
        key_forward(j).start()

    square = lax.broadcasted_iota(jnp.int32, (LANES, LANES), 0) == lax.broadcasted_iota(jnp.int32, (LANES, LANES), 1)

    def make_cols(j):
        def one(g):
            key_cols[j, g] = jnp.sum(jnp.where(square, key_rows[j, g], 0.0), axis=1, keepdims=True)

        each(0, groups, one)

    make_cols(0)

    size = min(2, groups)
    tile = size * LANES
    tiles = groups // size
    blocks = tile // cap

    def tile_rows(j, t):
        return rows[j, pl.ds(t * blocks, blocks)].reshape(tile, width)

    def score_chunk(j):
        def queries(qt):
            q = jnp.concatenate([key_rows[0, qt * size + i] for i in range(size)], axis=1)
            base = jnp.floor(q * (1.0 / total)) * total
            q_rows = tile_rows(0, qt)

            def keys(kt):
                c = jnp.concatenate([key_cols[j, kt * size + i] for i in range(size)], axis=0)
                dots = lax.dot_general(
                    tile_rows(j, kt), q_rows, (((1,), (1,)), ((), ())), preferred_element_type=jnp.float32
                )
                best = jnp.max(jnp.where((c < q) & (c >= base), dots, -1.0), axis=0, keepdims=True)
                for i in range(size):
                    part = best[:, i * LANES:(i + 1) * LANES]
                    scores[qt * size + i] = jnp.maximum(scores[qt * size + i], part)

            each(0, tiles, keys)

        each(0, tiles, queries)

    def clear(g):
        scores[g] = jnp.full((1, LANES), -1.0, jnp.float32)

    each(0, groups, clear)

    def arrive(j, k):
        if j:
            b = bits[level_of(j) - 1]
            forward_copy(j - b, b, k).wait_recv()
        else:
            rows_copy(k).wait_recv()
            rows[0, k] = unit(raw_rows[k])
        forward(level_of(j), j, k)

    def arrivals(level, k):
        for j in range(peers):
            if level_of(j) == level:
                arrive(j, k)

    levels = len(bits)

    def get_key_cols():
        for j in range(1, peers):
            key_forward(j).wait_recv()
            make_cols(j)

    if unrolled:
        queue = [0] + near + far
        for i in range(owners + LAG * (levels - 1)):
            for level in range(levels):
                if 0 <= i - LAG * level < owners and not (level == 0 and i == 0):
                    k = queue[i - LAG * level]
                    arrivals(level, k)
                    if level == 0 and k in far[:-WINDOW]:
                        rows_copy(k).wait_send()
                        rows_copy(k - WINDOW).start()
            if i == owners // 2:
                get_key_cols()
            if i == owners - 1:
                score_chunk(0)
    else:
        get_key_cols()
        for level in range(1, levels):
            arrivals(level, 0)

        def step(i):
            for level in range(levels):
                arrivals(level, owners - i)

        each(1, owners, step)
        score_chunk(0)
    for j in others:
        if level_of(j) == levels:
            each(0, owners, lambda k, j=j: arrive(j, k))
        score_chunk(j)

    each(1, owners, lambda k: back_copy(k).start())
    got_scores[0] = scores[0]
    lane_col = slot_col + ((rel_col.astype(jnp.int32) % per) * cap)
    each(1, owners, lambda k: back_copy(k).wait_recv())

    def pick(k, acc):
        kf = jnp.float32(k) if isinstance(k, int) else k.astype(jnp.float32)
        return jnp.where(rel_col == kf, got_scores[k], acc)

    found = jnp.zeros((docs, LANES), jnp.float32)
    if owners <= UNROLL_UP_TO:
        for k in range(owners):
            found = pick(k, found)
    else:
        found = lax.fori_loop(0, owners, pick, found)
    result = jnp.sum(jnp.where(lanes == lane_col, found, 0.0), axis=1, keepdims=True)
    out_ref[...] = jnp.sum(jnp.where(eye, result, 0.0), axis=0, keepdims=True)

    each(1, owners, lambda k: key_copy(k).wait_send())
    if unrolled:
        for k in near + far[-WINDOW:]:
            rows_copy(k).wait_send()
    else:
        each(1, owners, lambda k: rows_copy(k).wait_send())
    each(1, owners, lambda k: back_copy(k).wait_send())
    for j in range(1, peers):
        key_forward(j).wait_send()
        b = bits[level_of(j) - 1]
        each(0, owners, lambda k, j=j, b=b: forward_copy(j - b, b, k).wait_send())


def per_device(total, embeddings, cluster_id, rank):
    owners = lax.axis_size("docs")
    peers = lax.axis_size("split")
    docs, width = embeddings.shape
    cap = 2 * docs // owners
    cap = -(-cap // ROW_TILE) * ROW_TILE
    groups = owners * cap // LANES
    dma = pltpu.SemaphoreType.DMA
    vmem = pl.BlockSpec(memory_space=pltpu.VMEM)
    out = pl.pallas_call(
        functools.partial(kernel, owners, peers, cap, float(total)),
        out_shape=jax.ShapeDtypeStruct((1, docs), jnp.float32),
        in_specs=[pl.BlockSpec(memory_space=pltpu.HBM)] * 3,
        out_specs=vmem,
        scratch_shapes=[
            pltpu.VMEM((docs, width), embeddings.dtype),
            pltpu.VMEM((1, docs), jnp.int32),
            pltpu.VMEM((1, docs), jnp.int32),
            dma((3,)),
            pltpu.VMEM((owners, cap, width), embeddings.dtype),
            pltpu.VMEM((owners, cap, width), embeddings.dtype),
            pltpu.VMEM((peers, owners, cap, width), jnp.bfloat16),
            pltpu.VMEM((owners, 1, LANES), jnp.float32),
            pltpu.VMEM((owners, 1, LANES), jnp.float32),
            pltpu.VMEM((peers, groups, 1, LANES), jnp.float32),
            pltpu.VMEM((peers, groups, LANES, 1), jnp.float32),
            pltpu.VMEM((groups, 1, LANES), jnp.float32),
            pltpu.VMEM((owners, 1, LANES), jnp.float32),
            dma((owners,)), dma((owners,)),
            dma((peers, owners)), dma((peers, owners)),
            dma((owners,)), dma((owners,)),
            dma((peers,)), dma((peers,)),
            dma((owners,)), dma((owners,)),
        ],
        compiler_params=pltpu.CompilerParams(
            collective_id=0, has_side_effects=True, vmem_limit_bytes=127 * 512 * 1024
        ),
    )(embeddings, cluster_id.reshape(1, docs), rank.reshape(1, docs))
    return out.reshape(docs)


def solution(mesh):
    placed = (P(("docs", "split"), None), P(("docs", "split")), P(("docs", "split")))

    def run(embeddings, cluster_id, rank):
        return jax.shard_map(
            functools.partial(per_device, embeddings.shape[0]),
            mesh=mesh, in_specs=placed, out_specs=P(("docs", "split")), check_vma=False,
        )(embeddings, cluster_id, rank)

    return run
```

```python
import functools

import jax
import jax.numpy as jnp
from jax import lax
from jax.experimental import pallas as pl
from jax.experimental.pallas import tpu as pltpu
from jax.sharding import PartitionSpec as P

CL_DEV = 2
EPSILON = 1e-06
LANES = 128
ROW_TILE = 16
UNROLL_UP_TO = 8
MESH = pl.DeviceIdType.MESH


def xor(a, b, size):
    out, bit = 0, 1
    while bit < size:
        out = out + bit * (((a // bit) + (b // bit)) % 2)
        bit *= 2
    return out


def each(start, stop, body):
    if stop - start <= UNROLL_UP_TO:
        for i in range(start, stop):
            body(i)
    else:
        lax.fori_loop(start, stop, lambda i, c: (body(i), c)[1], 0)


def kernel(
    owners, pairs, cap, total,
    emb_hbm, cluster_hbm, rank_hbm, out_ref,
    emb_ref, cluster_ref, rank_ref, load_sems, send_rows, rows, send_keys, got_keys, key_rows, key_cols, scores,
    got_scores, own_sem, rows_out, rows_in, fwd_out, fwd_in, keys_out, keys_in, kfwd_out, kfwd_in, back_out, back_in,
):
    docs, width = emb_ref.shape
    per = LANES // cap
    groups = key_rows.shape[1]
    sources = owners * pairs
    me = lax.axis_index("docs")
    mine = lax.axis_index("split")
    pair, core = mine // 2, mine % 2
    first = (owners - owners // pairs) // 2
    is_owner = (me >= first) & (me < first + owners // pairs)
    my_owner = (me - first) * pairs + pair
    my_slot = me * pairs + pair
    my_rel = xor(me, jnp.where(is_owner, my_owner, 0), owners)

    loads = [
        pltpu.make_async_copy(src, dst, load_sems.at[i])
        for i, (src, dst) in enumerate(((cluster_hbm, cluster_ref), (rank_hbm, rank_ref), (emb_hbm, emb_ref)))
    ]
    for load in loads:
        load.start()

    def owner_device(k):
        o = xor(me, k, owners)
        return {"docs": first + o // pairs, "split": (o % pairs) * 2 + core}

    def not_self(k):
        return jnp.logical_not(is_owner & (my_rel == k))

    def to_owners(body):
        def one(k):
            @pl.when(not_self(k))
            def _():
                body(k)

        half = owners // 2

        def step(i):
            one(owners - 1 - i)
            one(half - 1 - i)

        each(0, half, step)

    def from_sources(body):
        def one(k):
            p = xor(my_owner, k, owners)
            for x in range(pairs):
                @pl.when(jnp.logical_not((p == me) & (pair == x)))
                def _():
                    body(p * pairs + x, k, {"docs": p, "split": x * 2 + core})

        half = owners // 2

        def step(i):
            one(owners - 1 - i)
            one(half - 1 - i)

        each(0, half, step)

    sibling = {"split": pair * 2 + (1 - core)}
    barrier = pltpu.get_barrier_semaphore()

    def greet(device):
        pl.semaphore_signal(barrier, inc=1, device_id=device, device_id_type=MESH)

    to_owners(lambda k: greet(owner_device(k)))

    @pl.when(is_owner)
    def _():
        greet(sibling)
        from_sources(lambda slot, k, device: greet(device))

    def copy(src, dst, out_sem, in_sem, device):
        return pltpu.make_async_remote_copy(
            src_ref=src, dst_ref=dst, send_sem=out_sem, recv_sem=in_sem, device_id=device, device_id_type=MESH
        )

    def rows_copy(k, slot):
        return copy(send_rows.at[k], rows.at[0, slot], rows_out.at[k], rows_in.at[slot], owner_device(k))

    def key_copy(k, slot):
        return copy(send_keys.at[k], got_keys.at[slot], keys_out.at[k], keys_in.at[slot], owner_device(k))

    def forward_copy(slot):
        return copy(rows.at[0, slot], rows.at[1, slot], fwd_out.at[slot], fwd_in.at[slot], sibling)

    key_forward = copy(key_rows.at[0], key_rows.at[1], kfwd_out, kfwd_in, sibling)

    def back_copy(slot, k, device):
        return copy(scores.at[slot // per], got_scores.at[k], back_out.at[slot], back_in.at[k], device)

    row_id = lax.broadcasted_iota(jnp.int32, (docs, docs), 0)
    lane_id = lax.broadcasted_iota(jnp.int32, (docs, docs), 1)
    eye = row_id == lane_id

    def column(row):
        return jnp.sum(jnp.where(eye, row, 0.0), axis=1, keepdims=True)

    loads[0].wait()
    loads[1].wait()
    cluster = cluster_ref[...]
    owner = lax.shift_right_logical(cluster, CL_DEV.bit_length() - 1)
    local = cluster - owner * CL_DEV
    key = (local + 1).astype(jnp.float32) * total + rank_ref[...].astype(jnp.float32)
    rel = jnp.bitwise_xor(owner, me).astype(jnp.float32)
    rel_col, key_col = column(rel), column(key)
    same = rel_col == rel
    before = jnp.sum(jnp.where(same & (row_id < lane_id), 1.0, 0.0), axis=0, keepdims=True)
    before_col = jnp.sum(jnp.where(same & (lane_id < row_id), 1.0, 0.0), axis=1, keepdims=True)
    target = (rel * cap + before).astype(jnp.int32)
    lanes = lax.broadcasted_iota(jnp.int32, (docs, LANES), 1)
    lane_col = before_col.astype(jnp.int32) + (my_slot % per) * cap
    placed = jnp.where(lanes == lane_col, key_col, 0.0)

    def number(k):
        return jnp.float32(k) if isinstance(k, int) else k.astype(jnp.float32)

    def put_keys(k):
        send_keys[k] = jnp.sum(jnp.where(rel_col == number(k), placed, 0.0), axis=0, keepdims=True)

    each(0, owners, put_keys)

    loads[2].wait()
    values = emb_ref[...].astype(jnp.float32)
    norm = jnp.sqrt(jnp.sum(values * values, axis=1, keepdims=True) + EPSILON)
    unit = (values * (1.0 / norm)).astype(jnp.bfloat16)
    slot_id = lax.broadcasted_iota(jnp.int32, (cap, docs), 0)

    @pl.when(is_owner)
    def _():
        pl.semaphore_wait(barrier, owners - 1 + sources - 1 + 1)

    @pl.when(jnp.logical_not(is_owner))
    def _():
        pl.semaphore_wait(barrier, owners)

    to_owners(lambda k: key_copy(k, my_slot).start())

    def send(i):
        for k in (owners - 1 - i, owners // 2 - 1 - i):
            pick = jnp.where(slot_id + k * cap == target, 1.0, 0.0).astype(jnp.bfloat16)
            send_rows[k] = jnp.dot(pick, unit, preferred_element_type=jnp.float32).astype(jnp.bfloat16)

            @pl.when(not_self(k))
            def _(k=k):
                rows_copy(k, my_slot).start()

    each(0, owners // 2, send)

    size = min(2, groups)
    tile = size * LANES
    tiles = groups // size
    blocks = tile // cap
    square = lax.broadcasted_iota(jnp.int32, (LANES, LANES), 0) == lax.broadcasted_iota(jnp.int32, (LANES, LANES), 1)

    def make_cols(j):
        def one(g):
            key_cols[j, g] = jnp.sum(jnp.where(square, key_rows[j, g], 0.0), axis=1, keepdims=True)

        each(0, groups, one)

    def tile_rows(j, t):
        return rows[j, pl.ds(t * blocks, blocks)].reshape(tile, width)

    def score_chunk(j):
        def queries(qt):
            q = jnp.concatenate([key_rows[0, qt * size + i] for i in range(size)], axis=1)
            base = jnp.floor(q * (1.0 / total)) * total
            q_rows = tile_rows(0, qt)

            def keys(kt):
                c = jnp.concatenate([key_cols[j, kt * size + i] for i in range(size)], axis=0)
                dots = lax.dot_general(
                    tile_rows(j, kt), q_rows, (((1,), (1,)), ((), ())), preferred_element_type=jnp.float32
                )
                best = jnp.max(jnp.where((c < q) & (c >= base), dots, -1.0), axis=0, keepdims=True)
                for i in range(size):
                    part = best[:, i * LANES:(i + 1) * LANES]
                    scores[qt * size + i] = jnp.maximum(scores[qt * size + i], part)

            each(0, tiles, keys)

        each(0, tiles, queries)

    @pl.when(is_owner)
    def _():
        keep_rows = pltpu.make_async_copy(send_rows.at[my_rel], rows.at[0, my_slot], own_sem.at[0])
        keep_keys = pltpu.make_async_copy(send_keys.at[my_rel], got_keys.at[my_slot], own_sem.at[1])
        keep_rows.start()
        keep_keys.start()

        def clear(g):
            scores[g] = jnp.full((1, LANES), -1.0, jnp.float32)

        each(0, groups, clear)
        keep_keys.wait()
        from_sources(lambda slot, k, device: key_copy(k, slot).wait_recv())

        def sum_keys(g):
            acc = got_keys[g * per]
            for i in range(1, per):
                acc = acc + got_keys[g * per + i]
            key_rows[0, g] = acc

        each(0, groups, sum_keys)
        key_forward.start()
        make_cols(0)
        keep_rows.wait()
        forward_copy(my_slot).start()

        def arrive(slot, k, device):
            rows_copy(k, slot).wait_recv()
            forward_copy(slot).start()

        from_sources(arrive)
        key_forward.wait_recv()
        make_cols(1)
        score_chunk(0)
        each(0, sources, lambda slot: forward_copy(slot).wait_recv())
        score_chunk(1)
        keep_scores = pltpu.make_async_copy(scores.at[my_slot // per], got_scores.at[my_rel], own_sem.at[2])
        keep_scores.start()
        from_sources(lambda slot, k, device: back_copy(slot, k, device).start())
        keep_scores.wait()

    to_owners(lambda k: back_copy(my_slot, k, owner_device(k)).wait_recv())

    def pick(k, acc):
        return jnp.where(rel_col == number(k), got_scores[k], acc)

    found = jnp.zeros((docs, LANES), jnp.float32)
    if owners <= UNROLL_UP_TO:
        for k in range(owners):
            found = pick(k, found)
    else:
        found = lax.fori_loop(0, owners, pick, found)
    result = jnp.sum(jnp.where(lanes == lane_col, found, 0.0), axis=1, keepdims=True)
    out_ref[...] = jnp.sum(jnp.where(eye, result, 0.0), axis=0, keepdims=True)

    def sent(k):
        key_copy(k, my_slot).wait_send()
        rows_copy(k, my_slot).wait_send()

    to_owners(sent)

    @pl.when(is_owner)
    def _():
        key_forward.wait_send()
        each(0, sources, lambda slot: forward_copy(slot).wait_send())
        from_sources(lambda slot, k, device: back_copy(slot, k, device).wait_send())


def per_device(total, embeddings, cluster_id, rank):
    owners = lax.axis_size("docs")
    pairs = lax.axis_size("split") // 2
    docs, width = embeddings.shape
    cap = 2 * docs // owners
    cap = -(-cap // ROW_TILE) * ROW_TILE
    sources = owners * pairs
    groups = sources * cap // LANES
    dma = pltpu.SemaphoreType.DMA
    out = pl.pallas_call(
        functools.partial(kernel, owners, pairs, cap, float(total)),
        out_shape=jax.ShapeDtypeStruct((1, docs), jnp.float32),
        in_specs=[pl.BlockSpec(memory_space=pltpu.HBM)] * 3,
        out_specs=pl.BlockSpec(memory_space=pltpu.VMEM),
        scratch_shapes=[
            pltpu.VMEM((docs, width), embeddings.dtype),
            pltpu.VMEM((1, docs), jnp.int32),
            pltpu.VMEM((1, docs), jnp.int32),
            dma((3,)),
            pltpu.VMEM((owners, cap, width), jnp.bfloat16),
            pltpu.VMEM((2, sources, cap, width), jnp.bfloat16),
            pltpu.VMEM((owners, 1, LANES), jnp.float32),
            pltpu.VMEM((sources, 1, LANES), jnp.float32),
            pltpu.VMEM((2, groups, 1, LANES), jnp.float32),
            pltpu.VMEM((2, groups, LANES, 1), jnp.float32),
            pltpu.VMEM((groups, 1, LANES), jnp.float32),
            pltpu.VMEM((owners, 1, LANES), jnp.float32),
            dma((3,)),
            dma((owners,)), dma((sources,)),
            dma((sources,)), dma((sources,)),
            dma((owners,)), dma((sources,)),
            dma, dma,
            dma((sources,)), dma((owners,)),
        ],
        compiler_params=pltpu.CompilerParams(
            collective_id=0, has_side_effects=True, vmem_limit_bytes=127 * 512 * 1024
        ),
    )(embeddings, cluster_id.reshape(1, docs), rank.reshape(1, docs))
    return out.reshape(docs)


def solution(mesh):
    placed = (P(("docs", "split"), None), P(("docs", "split")), P(("docs", "split")))

    def run(embeddings, cluster_id, rank):
        return jax.shard_map(
            functools.partial(per_device, embeddings.shape[0]),
            mesh=mesh, in_specs=placed, out_specs=P(("docs", "split")), check_vma=False,
        )(embeddings, cluster_id, rank)

    return run
```

```python
import functools

import jax
import jax.numpy as jnp
from jax import lax
from jax.experimental import pallas as pl
from jax.experimental.pallas import tpu as pltpu
from jax.sharding import PartitionSpec as P

CL_DEV = 2
EPSILON = 1e-06
LANES = 128
ROW_TILE = 16
UNROLL_UP_TO = 8
MESH = pl.DeviceIdType.MESH


def xor(a, b, size):
    out, bit = 0, 1
    while bit < size:
        out = out + bit * (((a // bit) + (b // bit)) % 2)
        bit *= 2
    return out


def each(start, stop, body):
    if stop - start <= UNROLL_UP_TO:
        for i in range(start, stop):
            body(i)
    else:
        lax.fori_loop(start, stop, lambda i, c: (body(i), c)[1], 0)


def kernel(
    owners, pairs, cap, total,
    emb_hbm, cluster_ref, rank_ref, out_ref,
    emb_ref, load_sem, send_rows, rows, send_keys, got_keys, key_rows, key_cols, scores,
    got_scores, own_sem, rows_out, rows_in, fwd_out, fwd_in, keys_out, keys_in, kfwd_out, kfwd_in, back_out, back_in,
):
    docs, width = emb_ref.shape
    per = LANES // cap
    groups = key_rows.shape[1]
    sources = owners * pairs
    me = lax.axis_index("docs")
    mine = lax.axis_index("split")
    pair, core = mine // 2, mine % 2
    first = (owners - owners // pairs) // 2
    is_owner = (me >= first) & (me < first + owners // pairs)
    my_owner = (me - first) * pairs + pair
    half = owners // 2

    def distance(i):
        return owners - 1 - i // 2 - (i % 2) * half

    def turn(d):
        near = 1 - d // half
        return 2 * (owners - 1 - near * half - d) + near

    my_turn = turn(xor(me, jnp.where(is_owner, my_owner, 0), owners))

    load = pltpu.make_async_copy(emb_hbm, emb_ref, load_sem)
    load.start()

    def owner_device(i):
        o = xor(me, distance(i), owners)
        return {"docs": first + o // pairs, "split": (o % pairs) * 2 + core}

    def not_self(i):
        return jnp.logical_not(is_owner & (my_turn == i))

    def slot_of(i):
        return i * pairs + pair

    def to_owners(body):
        def one(i):
            @pl.when(not_self(i))
            def _():
                body(i)

        each(0, owners, one)

    def from_sources(body, start=0, stop=owners):
        def one(i):
            p = xor(my_owner, distance(i), owners)
            for x in range(pairs):
                @pl.when(jnp.logical_not((p == me) & (pair == x)))
                def _():
                    body(i * pairs + x, i, {"docs": p, "split": x * 2 + core})

        each(start, stop, one)

    sibling = {"split": pair * 2 + (1 - core)}
    barrier = pltpu.get_barrier_semaphore()

    def greet(device):
        pl.semaphore_signal(barrier, inc=1, device_id=device, device_id_type=MESH)

    to_owners(lambda k: greet(owner_device(k)))

    @pl.when(is_owner)
    def _():
        greet(sibling)
        from_sources(lambda slot, k, device: greet(device))

    def copy(src, dst, out_sem, in_sem, device):
        return pltpu.make_async_remote_copy(
            src_ref=src, dst_ref=dst, send_sem=out_sem, recv_sem=in_sem, device_id=device, device_id_type=MESH
        )

    def rows_copy(k, slot):
        return copy(send_rows.at[k], rows.at[0, slot], rows_out.at[k], rows_in.at[slot], owner_device(k))

    def key_copy(k, slot):
        return copy(send_keys.at[k], got_keys.at[slot], keys_out.at[k], keys_in.at[slot], owner_device(k))

    def forward_copy(slot):
        return copy(rows.at[0, slot], rows.at[1, slot], fwd_out.at[slot], fwd_in.at[slot], sibling)

    key_forward = copy(key_rows.at[0], key_rows.at[1], kfwd_out, kfwd_in, sibling)

    def back_copy(slot, k, device):
        return copy(scores.at[slot // per], got_scores.at[k], back_out.at[slot], back_in.at[k], device)

    row_id = lax.broadcasted_iota(jnp.int32, (docs, docs), 0)
    lane_id = lax.broadcasted_iota(jnp.int32, (docs, docs), 1)
    eye = row_id == lane_id

    def column(row):
        return jnp.sum(jnp.where(eye, row, 0.0), axis=1, keepdims=True)

    cluster = cluster_ref[...]
    owner = lax.shift_right_logical(cluster, CL_DEV.bit_length() - 1)
    local = cluster - owner * CL_DEV
    key = (local + 1).astype(jnp.float32) * total + rank_ref[...].astype(jnp.float32)
    apart = jnp.bitwise_xor(owner, me)
    turns = jnp.where(apart >= half, 2 * (owners - 1 - apart), 2 * (half - 1 - apart) + 1)
    rel = turns.astype(jnp.float32)
    rel_col, key_col = column(rel), column(key)
    same = rel_col == rel
    before = jnp.sum(jnp.where(same & (row_id < lane_id), 1.0, 0.0), axis=0, keepdims=True)
    before_col = jnp.sum(jnp.where(same & (lane_id < row_id), 1.0, 0.0), axis=1, keepdims=True)
    target = (rel * cap + before).astype(jnp.int32)
    lanes = lax.broadcasted_iota(jnp.int32, (docs, LANES), 1)
    lane_col = before_col.astype(jnp.int32) + jnp.bitwise_and(slot_of(rel_col.astype(jnp.int32)), per - 1) * cap
    placed = jnp.where(lanes == lane_col, key_col, 0.0)

    def number(k):
        return jnp.float32(k) if isinstance(k, int) else k.astype(jnp.float32)

    def put_keys(k):
        send_keys[k] = jnp.sum(jnp.where(rel_col == number(k), placed, 0.0), axis=0, keepdims=True)

    each(0, owners, put_keys)

    load.wait()
    values = emb_ref[...].astype(jnp.float32)
    norm = jnp.sqrt(jnp.sum(values * values, axis=1, keepdims=True) + EPSILON)
    unit = (values * (1.0 / norm)).astype(jnp.bfloat16)
    slot_id = lax.broadcasted_iota(jnp.int32, (cap, docs), 0)

    @pl.when(is_owner)
    def _():
        pl.semaphore_wait(barrier, owners - 1 + sources - 1 + 1)

    @pl.when(jnp.logical_not(is_owner))
    def _():
        pl.semaphore_wait(barrier, owners)

    to_owners(lambda i: key_copy(i, slot_of(i)).start())

    def send(i):
        pick = jnp.where(slot_id + i * cap == target, 1.0, 0.0).astype(jnp.bfloat16)
        send_rows[i] = jnp.dot(pick, unit, preferred_element_type=jnp.float32).astype(jnp.bfloat16)

        @pl.when(not_self(i))
        def _():
            rows_copy(i, slot_of(i)).start()

    each(0, owners, send)

    size = min(2, groups)
    tile = size * LANES
    tiles = groups // size
    blocks = tile // cap
    square = lax.broadcasted_iota(jnp.int32, (LANES, LANES), 0) == lax.broadcasted_iota(jnp.int32, (LANES, LANES), 1)

    def make_cols(j):
        def one(g):
            key_cols[j, g] = jnp.sum(jnp.where(square, key_rows[j, g], 0.0), axis=1, keepdims=True)

        each(0, groups, one)

    def tile_rows(j, t, n=1):
        return rows[j, pl.ds(t * blocks, n * blocks)].reshape(n * tile, width)

    def score(j, qt, kt, n=1):
        q = jnp.concatenate([key_rows[0, qt * size + i] for i in range(size)], axis=1)
        base = jnp.floor(q * (1.0 / total)) * total
        c = jnp.concatenate([key_cols[j, kt * size + i] for i in range(n * size)], axis=0)
        dots = lax.dot_general(
            tile_rows(j, kt, n), tile_rows(0, qt), (((1,), (1,)), ((), ())), preferred_element_type=jnp.float32
        )
        best = jnp.max(jnp.where((c < q) & (c >= base), dots, -1.0), axis=0, keepdims=True)
        for i in range(size):
            part = best[:, i * LANES:(i + 1) * LANES]
            scores[qt * size + i] = jnp.maximum(scores[qt * size + i], part)

    @pl.when(is_owner)
    def _():
        keep_rows = pltpu.make_async_copy(send_rows.at[my_turn], rows.at[0, slot_of(my_turn)], own_sem.at[0])
        keep_keys = pltpu.make_async_copy(send_keys.at[my_turn], got_keys.at[slot_of(my_turn)], own_sem.at[1])
        keep_rows.start()
        keep_keys.start()

        def clear(g):
            scores[g] = jnp.full((1, LANES), -1.0, jnp.float32)

        each(0, groups, clear)
        keep_keys.wait()
        from_sources(lambda slot, k, device: key_copy(k, slot).wait_recv())

        def sum_keys(g):
            acc = got_keys[g * per]
            for i in range(1, per):
                acc = acc + got_keys[g * per + i]
            key_rows[0, g] = acc

        each(0, groups, sum_keys)
        key_forward.start()
        make_cols(0)
        keep_rows.wait()
        forward_copy(slot_of(my_turn)).start()

        def arrive(slot, k, device):
            rows_copy(k, slot).wait_recv()
            forward_copy(slot).start()

        def forwarded(start, stop):
            each(start, stop, lambda slot: forward_copy(slot).wait_recv())

        if tiles == 2:
            middle = half + 1
            from_sources(arrive, 0, half)
            key_forward.wait_recv()
            make_cols(1)
            score(0, 0, 0)
            from_sources(arrive, half, middle)
            forwarded(0, blocks)
            score(1, 0, 0)
            from_sources(arrive, middle)
            score(0, 1, 0, 2)
            score(0, 0, 1)
            score(1, 1, 0)
            forwarded(blocks, sources)
            score(1, 1, 1)
            score(1, 0, 1)
        else:
            from_sources(arrive)
            key_forward.wait_recv()
            make_cols(1)
            forwarded(0, sources)
            for j in range(2):
                each(0, tiles, lambda qt, j=j: each(0, tiles, lambda kt: score(j, qt, kt)))
        keep_scores = pltpu.make_async_copy(scores.at[slot_of(my_turn) // per], got_scores.at[my_turn], own_sem.at[2])
        keep_scores.start()
        from_sources(lambda slot, k, device: back_copy(slot, k, device).start())
        keep_scores.wait()

    to_owners(lambda k: back_copy(slot_of(k), k, owner_device(k)).wait_recv())

    def pick(k, acc):
        return jnp.where(rel_col == number(k), got_scores[k], acc)

    found = jnp.zeros((docs, LANES), jnp.float32)
    if owners <= UNROLL_UP_TO:
        for k in range(owners):
            found = pick(k, found)
    else:
        found = lax.fori_loop(0, owners, pick, found)
    result = jnp.sum(jnp.where(lanes == lane_col, found, 0.0), axis=1, keepdims=True)
    out_ref[...] = jnp.sum(jnp.where(eye, result, 0.0), axis=0, keepdims=True)

    def sent(k):
        key_copy(k, slot_of(k)).wait_send()
        rows_copy(k, slot_of(k)).wait_send()

    to_owners(sent)

    @pl.when(is_owner)
    def _():
        key_forward.wait_send()
        each(0, sources, lambda slot: forward_copy(slot).wait_send())
        from_sources(lambda slot, k, device: back_copy(slot, k, device).wait_send())


def per_device(total, embeddings, cluster_id, rank):
    owners = lax.axis_size("docs")
    pairs = lax.axis_size("split") // 2
    docs, width = embeddings.shape
    cap = 2 * docs // owners
    cap = -(-cap // ROW_TILE) * ROW_TILE
    sources = owners * pairs
    groups = sources * cap // LANES
    dma = pltpu.SemaphoreType.DMA
    out = pl.pallas_call(
        functools.partial(kernel, owners, pairs, cap, float(total)),
        out_shape=jax.ShapeDtypeStruct((1, docs), jnp.float32),
        in_specs=[pl.BlockSpec(memory_space=pl.ANY)] + [pl.BlockSpec(memory_space=pltpu.VMEM)] * 2,
        out_specs=pl.BlockSpec(memory_space=pltpu.VMEM),
        scratch_shapes=[
            pltpu.VMEM((docs, width), embeddings.dtype),
            dma,
            pltpu.VMEM((owners, cap, width), jnp.bfloat16),
            pltpu.VMEM((2, sources, cap, width), jnp.bfloat16),
            pltpu.VMEM((owners, 1, LANES), jnp.float32),
            pltpu.VMEM((sources, 1, LANES), jnp.float32),
            pltpu.VMEM((2, groups, 1, LANES), jnp.float32),
            pltpu.VMEM((2, groups, LANES, 1), jnp.float32),
            pltpu.VMEM((groups, 1, LANES), jnp.float32),
            pltpu.VMEM((owners, 1, LANES), jnp.float32),
            dma((3,)),
            dma((owners,)), dma((sources,)),
            dma((sources,)), dma((sources,)),
            dma((owners,)), dma((sources,)),
            dma, dma,
            dma((sources,)), dma((owners,)),
        ],
        compiler_params=pltpu.CompilerParams(
            collective_id=0, has_side_effects=True, vmem_limit_bytes=860 * 64 * 1024
        ),
    )(embeddings, cluster_id.reshape(1, docs), rank.reshape(1, docs))
    return out.reshape(docs)


def solution(mesh):
    placed = (P(("docs", "split"), None), P(("docs", "split")), P(("docs", "split")))

    def run(embeddings, cluster_id, rank):
        return jax.shard_map(
            functools.partial(per_device, embeddings.shape[0]),
            mesh=mesh, in_specs=placed, out_specs=P(("docs", "split")), check_vma=False,
        )(embeddings, cluster_id, rank)

    return run
```

```python
import functools

import jax
import jax.numpy as jnp
from jax import lax
from jax.experimental import pallas as pl
from jax.experimental.pallas import tpu as pltpu
from jax.sharding import PartitionSpec as P

CL_DEV = 2
EPSILON = 1e-06
LANES = 128
ROW_TILE = 16
UNROLL_UP_TO = 8
MESH = pl.DeviceIdType.MESH


def xor(a, b, size):
    out, bit = 0, 1
    while bit < size:
        out = out + bit * (((a // bit) + (b // bit)) % 2)
        bit *= 2
    return out


def each(start, stop, body):
    if stop - start <= UNROLL_UP_TO:
        for i in range(start, stop):
            body(i)
    else:
        lax.fori_loop(start, stop, lambda i, c: (body(i), c)[1], 0)


def kernel(
    owners, pairs, cap, total,
    emb_hbm, cluster_ref, rank_ref, out_ref,
    emb_ref, load_sem, send_rows, rows, send_keys, got_keys, key_rows, key_cols, scores,
    got_scores, own_sem, rows_out, rows_in, fwd_out, fwd_in, keys_out, keys_in, kfwd_out, kfwd_in, back_out, back_in,
):
    docs, width = emb_ref.shape
    per = LANES // cap
    groups = key_rows.shape[1]
    sources = owners * pairs
    me = lax.axis_index("docs")
    mine = lax.axis_index("split")
    pair, core = mine // 2, mine % 2
    first = (owners - owners // pairs) // 2
    is_owner = (me >= first) & (me < first + owners // pairs)
    my_owner = (me - first) * pairs + pair
    half = owners // 2

    def distance(i):
        return owners - 1 - i

    my_turn = distance(xor(me, jnp.where(is_owner, my_owner, 0), owners))

    load = pltpu.make_async_copy(emb_hbm, emb_ref, load_sem)
    load.start()

    def owner_device(i):
        o = xor(me, distance(i), owners)
        return {"docs": first + o // pairs, "split": (o % pairs) * 2 + core}

    def not_self(i):
        return jnp.logical_not(is_owner & (my_turn == i))

    def slot_of(i):
        return i * pairs + pair

    def to_owners(body):
        def one(i):
            @pl.when(not_self(i))
            def _():
                body(i)

        each(0, owners, one)

    def from_sources(body, start=0, stop=owners):
        def one(i):
            p = xor(my_owner, distance(i), owners)
            for x in range(pairs):
                @pl.when(jnp.logical_not((p == me) & (pair == x)))
                def _():
                    body(i * pairs + x, i, {"docs": p, "split": x * 2 + core})

        each(start, stop, one)

    sibling = {"split": pair * 2 + (1 - core)}
    barrier = pltpu.get_barrier_semaphore()

    def greet(device):
        pl.semaphore_signal(barrier, inc=1, device_id=device, device_id_type=MESH)

    to_owners(lambda k: greet(owner_device(k)))

    @pl.when(is_owner)
    def _():
        greet(sibling)
        from_sources(lambda slot, k, device: greet(device))

    def copy(src, dst, out_sem, in_sem, device):
        return pltpu.make_async_remote_copy(
            src_ref=src, dst_ref=dst, send_sem=out_sem, recv_sem=in_sem, device_id=device, device_id_type=MESH
        )

    def rows_copy(k, slot):
        return copy(send_rows.at[k], rows.at[0, slot], rows_out.at[k], rows_in.at[slot], owner_device(k))

    def key_copy(k, slot):
        return copy(send_keys.at[k], got_keys.at[slot], keys_out.at[k], keys_in.at[slot], owner_device(k))

    def forward_copy(slot):
        return copy(rows.at[0, slot], rows.at[1, slot], fwd_out.at[slot], fwd_in.at[slot], sibling)

    key_forward = copy(key_rows.at[0], key_rows.at[1], kfwd_out, kfwd_in, sibling)

    def back_copy(slot, k, device):
        return copy(scores.at[slot // per], got_scores.at[k], back_out.at[slot], back_in.at[k], device)

    row_id = lax.broadcasted_iota(jnp.int32, (docs, docs), 0)
    lane_id = lax.broadcasted_iota(jnp.int32, (docs, docs), 1)
    eye = row_id == lane_id

    def column(row):
        return jnp.sum(jnp.where(eye, row, 0.0), axis=1, keepdims=True)

    cluster = cluster_ref[...]
    owner = lax.shift_right_logical(cluster, CL_DEV.bit_length() - 1)
    local = cluster - owner * CL_DEV
    key = (local + 1).astype(jnp.float32) * total + rank_ref[...].astype(jnp.float32)
    rel = distance(jnp.bitwise_xor(owner, me)).astype(jnp.float32)
    rel_col, key_col = column(rel), column(key)
    same = rel_col == rel
    before = jnp.sum(jnp.where(same & (row_id < lane_id), 1.0, 0.0), axis=0, keepdims=True)
    before_col = jnp.sum(jnp.where(same & (lane_id < row_id), 1.0, 0.0), axis=1, keepdims=True)
    target = (rel * cap + before).astype(jnp.int32)
    lanes = lax.broadcasted_iota(jnp.int32, (docs, LANES), 1)
    lane_col = before_col.astype(jnp.int32) + jnp.bitwise_and(slot_of(rel_col.astype(jnp.int32)), per - 1) * cap
    placed = jnp.where(lanes == lane_col, key_col, 0.0)

    def number(k):
        return jnp.float32(k) if isinstance(k, int) else k.astype(jnp.float32)

    def put_keys(k):
        send_keys[k] = jnp.sum(jnp.where(rel_col == number(k), placed, 0.0), axis=0, keepdims=True)

    each(0, owners, put_keys)

    load.wait()
    values = emb_ref[...].astype(jnp.float32)
    norm = jnp.sqrt(jnp.sum(values * values, axis=1, keepdims=True) + EPSILON)
    unit = (values * (1.0 / norm)).astype(jnp.bfloat16)
    slot_id = lax.broadcasted_iota(jnp.int32, (cap, docs), 0)

    @pl.when(is_owner)
    def _():
        pl.semaphore_wait(barrier, owners - 1 + sources - 1 + 1)

    @pl.when(jnp.logical_not(is_owner))
    def _():
        pl.semaphore_wait(barrier, owners)

    to_owners(lambda i: key_copy(i, slot_of(i)).start())

    def send(i):
        pick = jnp.where(slot_id + i * cap == target, 1.0, 0.0).astype(jnp.bfloat16)
        send_rows[i] = jnp.dot(pick, unit, preferred_element_type=jnp.float32).astype(jnp.bfloat16)

        @pl.when(not_self(i))
        def _():
            rows_copy(i, slot_of(i)).start()

    each(0, owners, send)

    size = min(2, groups)
    tile = size * LANES
    tiles = groups // size
    blocks = tile // cap
    square = lax.broadcasted_iota(jnp.int32, (LANES, LANES), 0) == lax.broadcasted_iota(jnp.int32, (LANES, LANES), 1)

    def make_cols(j):
        def one(g):
            key_cols[j, g] = jnp.sum(jnp.where(square, key_rows[j, g], 0.0), axis=1, keepdims=True)

        each(0, groups, one)

    def tile_rows(j, t, n=1):
        return rows[j, pl.ds(t * blocks, n * blocks)].reshape(n * tile, width)

    def score(j, qt, kt, n=1):
        q = jnp.concatenate([key_rows[0, qt * size + i] for i in range(size)], axis=1)
        base = jnp.floor(q * (1.0 / total)) * total
        c = jnp.concatenate([key_cols[j, kt * size + i] for i in range(n * size)], axis=0)
        dots = lax.dot_general(
            tile_rows(j, kt, n), tile_rows(0, qt), (((1,), (1,)), ((), ())), preferred_element_type=jnp.float32
        )
        best = jnp.max(jnp.where((c < q) & (c >= base), dots, -1.0), axis=0, keepdims=True)
        for i in range(size):
            part = best[:, i * LANES:(i + 1) * LANES]
            scores[qt * size + i] = jnp.maximum(scores[qt * size + i], part)

    @pl.when(is_owner)
    def _():
        keep_rows = pltpu.make_async_copy(send_rows.at[my_turn], rows.at[0, slot_of(my_turn)], own_sem.at[0])
        keep_keys = pltpu.make_async_copy(send_keys.at[my_turn], got_keys.at[slot_of(my_turn)], own_sem.at[1])
        keep_rows.start()
        keep_keys.start()

        def clear(g):
            scores[g] = jnp.full((1, LANES), -1.0, jnp.float32)

        each(0, groups, clear)
        keep_keys.wait()
        from_sources(lambda slot, k, device: key_copy(k, slot).wait_recv())

        def sum_keys(g):
            acc = got_keys[g * per]
            for i in range(1, per):
                acc = acc + got_keys[g * per + i]
            key_rows[0, g] = acc

        each(0, groups, sum_keys)
        key_forward.start()
        make_cols(0)
        keep_rows.wait()
        forward_copy(slot_of(my_turn)).start()

        def arrive(slot, k, device):
            rows_copy(k, slot).wait_recv()
            forward_copy(slot).start()

        def send_back(start, stop):
            from_sources(lambda slot, k, device: back_copy(slot, k, device).start(), start, stop)

        def forwarded(start, stop):
            each(start, stop, lambda slot: forward_copy(slot).wait_recv())

        if tiles == 2:
            middle = half + 1
            from_sources(arrive, 0, half)
            key_forward.wait_recv()
            make_cols(1)
            score(0, 0, 0)
            from_sources(arrive, half, middle)
            forwarded(0, blocks)
            score(1, 0, 0)
            from_sources(arrive, middle)
            score(0, 1, 0, 2)
            score(0, 0, 1)
            score(1, 1, 0)
            forwarded(blocks, sources)
            score(1, 0, 1)
            send_back(0, half)
            score(1, 1, 1)
            send_back(half, owners)
        else:
            from_sources(arrive)
            key_forward.wait_recv()
            make_cols(1)
            forwarded(0, sources)
            for j in range(2):
                each(0, tiles, lambda qt, j=j: each(0, tiles, lambda kt: score(j, qt, kt)))
            send_back(0, owners)
        keep_scores = pltpu.make_async_copy(scores.at[slot_of(my_turn) // per], got_scores.at[my_turn], own_sem.at[2])
        keep_scores.start()
        keep_scores.wait()

    to_owners(lambda k: back_copy(slot_of(k), k, owner_device(k)).wait_recv())

    def pick(k, acc):
        return jnp.where(rel_col == number(k), got_scores[k], acc)

    found = jnp.zeros((docs, LANES), jnp.float32)
    if owners <= UNROLL_UP_TO:
        for k in range(owners):
            found = pick(k, found)
    else:
        found = lax.fori_loop(0, owners, pick, found)
    result = jnp.sum(jnp.where(lanes == lane_col, found, 0.0), axis=1, keepdims=True)
    out_ref[...] = jnp.sum(jnp.where(eye, result, 0.0), axis=0, keepdims=True)

    def sent(k):
        key_copy(k, slot_of(k)).wait_send()
        rows_copy(k, slot_of(k)).wait_send()

    to_owners(sent)

    @pl.when(is_owner)
    def _():
        key_forward.wait_send()
        each(0, sources, lambda slot: forward_copy(slot).wait_send())
        from_sources(lambda slot, k, device: back_copy(slot, k, device).wait_send())


def per_device(total, embeddings, cluster_id, rank):
    owners = lax.axis_size("docs")
    pairs = lax.axis_size("split") // 2
    docs, width = embeddings.shape
    cap = 2 * docs // owners
    cap = -(-cap // ROW_TILE) * ROW_TILE
    sources = owners * pairs
    groups = sources * cap // LANES
    dma = pltpu.SemaphoreType.DMA
    out = pl.pallas_call(
        functools.partial(kernel, owners, pairs, cap, float(total)),
        out_shape=jax.ShapeDtypeStruct((1, docs), jnp.float32),
        in_specs=[pl.BlockSpec(memory_space=pl.ANY)] + [pl.BlockSpec(memory_space=pltpu.VMEM)] * 2,
        out_specs=pl.BlockSpec(memory_space=pltpu.VMEM),
        scratch_shapes=[
            pltpu.VMEM((docs, width), embeddings.dtype),
            dma,
            pltpu.VMEM((owners, cap, width), jnp.bfloat16),
            pltpu.VMEM((2, sources, cap, width), jnp.bfloat16),
            pltpu.VMEM((owners, 1, LANES), jnp.float32),
            pltpu.VMEM((sources, 1, LANES), jnp.float32),
            pltpu.VMEM((2, groups, 1, LANES), jnp.float32),
            pltpu.VMEM((2, groups, LANES, 1), jnp.float32),
            pltpu.VMEM((groups, 1, LANES), jnp.float32),
            pltpu.VMEM((owners, 1, LANES), jnp.float32),
            dma((3,)),
            dma((owners,)), dma((sources,)),
            dma((sources,)), dma((sources,)),
            dma((owners,)), dma((sources,)),
            dma, dma,
            dma((sources,)), dma((owners,)),
        ],
        compiler_params=pltpu.CompilerParams(
            collective_id=0, has_side_effects=True, vmem_limit_bytes=860 * 64 * 1024
        ),
    )(embeddings, cluster_id.reshape(1, docs), rank.reshape(1, docs))
    return out.reshape(docs)


def solution(mesh):
    placed = (P(("docs", "split"), None), P(("docs", "split")), P(("docs", "split")))

    def run(embeddings, cluster_id, rank):
        return jax.shard_map(
            functools.partial(per_device, embeddings.shape[0]),
            mesh=mesh, in_specs=placed, out_specs=P(("docs", "split")), check_vma=False,
        )(embeddings, cluster_id, rank)

    return run
```

```python
import functools

import jax
import jax.numpy as jnp
from jax import lax
from jax.experimental import pallas as pl
from jax.experimental.pallas import tpu as pltpu
from jax.sharding import PartitionSpec as P

CL_DEV = 2
EPSILON = 1e-06
LANES = 128
ROW_TILE = 16
UNROLL_UP_TO = 8
MESH = pl.DeviceIdType.MESH


def xor(a, b, size):
    out, bit = 0, 1
    while bit < size:
        out = out + bit * (((a // bit) + (b // bit)) % 2)
        bit *= 2
    return out


def each(start, stop, body):
    if stop - start <= UNROLL_UP_TO:
        for i in range(start, stop):
            body(i)
    else:
        lax.fori_loop(start, stop, lambda i, c: (body(i), c)[1], 0)


def kernel(
    owners, pairs, cap, total,
    emb_hbm, cluster_ref, rank_ref, out_ref,
    emb_ref, load_sem, send_rows, rows, send_keys, got_keys, key_rows, key_cols, scores,
    got_scores, own_sem, rows_out, rows_in, fwd_out, fwd_in, keys_out, keys_in, kfwd_out, kfwd_in, back_out, back_in,
):
    docs, width = emb_ref.shape
    per = LANES // cap
    groups = key_rows.shape[1]
    sources = owners * pairs
    me = lax.axis_index("docs")
    mine = lax.axis_index("split")
    pair, core = mine // 2, mine % 2
    first = (owners - owners // pairs) // 2
    is_owner = (me >= first) & (me < first + owners // pairs)
    my_owner = (me - first) * pairs + pair
    half = owners // 2

    def distance(i):
        return owners - 1 - i // 2 - (i % 2) * half

    def turn(d):
        near = 1 - d // half
        return 2 * (owners - 1 - near * half - d) + near

    my_turn = turn(xor(me, jnp.where(is_owner, my_owner, 0), owners))

    load = pltpu.make_async_copy(emb_hbm, emb_ref, load_sem)
    load.start()

    def owner_device(i):
        o = xor(me, distance(i), owners)
        return {"docs": first + o // pairs, "split": (o % pairs) * 2 + core}

    def not_self(i):
        return jnp.logical_not(is_owner & (my_turn == i))

    def slot_of(i):
        return i * pairs + pair

    def to_owners(body):
        def one(i):
            @pl.when(not_self(i))
            def _():
                body(i)

        each(0, owners, one)

    def from_sources(body, start=0, stop=owners):
        def one(i):
            p = xor(my_owner, distance(i), owners)
            for x in range(pairs):
                @pl.when(jnp.logical_not((p == me) & (pair == x)))
                def _():
                    body(i * pairs + x, i, {"docs": p, "split": x * 2 + core})

        each(start, stop, one)

    sibling = {"split": pair * 2 + (1 - core)}
    barrier = pltpu.get_barrier_semaphore()

    def greet(device):
        pl.semaphore_signal(barrier, inc=1, device_id=device, device_id_type=MESH)

    to_owners(lambda k: greet(owner_device(k)))

    @pl.when(is_owner)
    def _():
        greet(sibling)
        from_sources(lambda slot, k, device: greet(device))

    def copy(src, dst, out_sem, in_sem, device):
        return pltpu.make_async_remote_copy(
            src_ref=src, dst_ref=dst, send_sem=out_sem, recv_sem=in_sem, device_id=device, device_id_type=MESH
        )

    def rows_copy(k, slot):
        return copy(send_rows.at[k], rows.at[0, slot], rows_out.at[k], rows_in.at[slot], owner_device(k))

    def key_copy(k, slot):
        return copy(send_keys.at[k], got_keys.at[slot], keys_out.at[k], keys_in.at[slot], owner_device(k))

    def forward_copy(slot):
        return copy(rows.at[0, slot], rows.at[1, slot], fwd_out.at[slot], fwd_in.at[slot], sibling)

    key_forward = copy(key_rows.at[0], key_rows.at[1], kfwd_out, kfwd_in, sibling)

    def back_copy(slot, k, device):
        return copy(scores.at[slot // per], got_scores.at[k], back_out.at[slot], back_in.at[k], device)

    row_id = lax.broadcasted_iota(jnp.int32, (docs, docs), 0)
    lane_id = lax.broadcasted_iota(jnp.int32, (docs, docs), 1)
    eye = row_id == lane_id

    def column(row):
        return jnp.sum(jnp.where(eye, row, 0.0), axis=1, keepdims=True)

    cluster = cluster_ref[...]
    owner = lax.shift_right_logical(cluster, CL_DEV.bit_length() - 1)
    local = cluster - owner * CL_DEV
    key = (local + 1).astype(jnp.float32) * total + rank_ref[...].astype(jnp.float32)
    apart = jnp.bitwise_xor(owner, me)
    turns = jnp.where(apart >= half, 2 * (owners - 1 - apart), 2 * (half - 1 - apart) + 1)
    rel = turns.astype(jnp.float32)
    rel_col, key_col = column(rel), column(key)
    same = rel_col == rel
    before = jnp.sum(jnp.where(same & (row_id < lane_id), 1.0, 0.0), axis=0, keepdims=True)
    before_col = jnp.sum(jnp.where(same & (lane_id < row_id), 1.0, 0.0), axis=1, keepdims=True)
    target = (rel * cap + before).astype(jnp.int32)
    lanes = lax.broadcasted_iota(jnp.int32, (docs, LANES), 1)
    lane_col = before_col.astype(jnp.int32) + jnp.bitwise_and(slot_of(rel_col.astype(jnp.int32)), per - 1) * cap
    placed = jnp.where(lanes == lane_col, key_col, 0.0)

    def number(k):
        return jnp.float32(k) if isinstance(k, int) else k.astype(jnp.float32)

    def put_keys(k):
        send_keys[k] = jnp.sum(jnp.where(rel_col == number(k), placed, 0.0), axis=0, keepdims=True)

    each(0, owners, put_keys)

    load.wait()
    values = emb_ref[...].astype(jnp.float32)
    norm = jnp.sqrt(jnp.sum(values * values, axis=1, keepdims=True) + EPSILON)
    unit = (values * (1.0 / norm)).astype(jnp.bfloat16)
    slot_id = lax.broadcasted_iota(jnp.int32, (cap, docs), 0)

    @pl.when(is_owner)
    def _():
        pl.semaphore_wait(barrier, owners - 1 + sources - 1 + 1)

    @pl.when(jnp.logical_not(is_owner))
    def _():
        pl.semaphore_wait(barrier, owners)

    def send(i):
        pick = jnp.where(slot_id + i * cap == target, 1.0, 0.0).astype(jnp.bfloat16)
        send_rows[i] = jnp.dot(pick, unit, preferred_element_type=jnp.float32).astype(jnp.bfloat16)

        @pl.when(not_self(i))
        def _():
            rows_copy(i, slot_of(i)).start()

    each(0, 2, send)
    to_owners(lambda i: key_copy(i, slot_of(i)).start())
    each(2, owners, send)

    size = min(2, groups)
    tile = size * LANES
    tiles = groups // size
    blocks = tile // cap
    square = lax.broadcasted_iota(jnp.int32, (LANES, LANES), 0) == lax.broadcasted_iota(jnp.int32, (LANES, LANES), 1)

    def make_cols(j):
        def one(g):
            key_cols[j, g] = jnp.sum(jnp.where(square, key_rows[j, g], 0.0), axis=1, keepdims=True)

        each(0, groups, one)

    def tile_rows(j, t, n=1):
        return rows[j, pl.ds(t * blocks, n * blocks)].reshape(n * tile, width)

    def score(j, qt, kt, n=1):
        q = jnp.concatenate([key_rows[0, qt * size + i] for i in range(size)], axis=1)
        base = jnp.floor(q * (1.0 / total)) * total
        c = jnp.concatenate([key_cols[j, kt * size + i] for i in range(n * size)], axis=0)
        dots = lax.dot_general(
            tile_rows(j, kt, n), tile_rows(0, qt), (((1,), (1,)), ((), ())), preferred_element_type=jnp.float32
        )
        best = jnp.max(jnp.where((c < q) & (c >= base), dots, -1.0), axis=0, keepdims=True)
        for i in range(size):
            part = best[:, i * LANES:(i + 1) * LANES]
            scores[qt * size + i] = jnp.maximum(scores[qt * size + i], part)

    @pl.when(is_owner)
    def _():
        keep_rows = pltpu.make_async_copy(send_rows.at[my_turn], rows.at[0, slot_of(my_turn)], own_sem.at[0])
        keep_keys = pltpu.make_async_copy(send_keys.at[my_turn], got_keys.at[slot_of(my_turn)], own_sem.at[1])
        keep_rows.start()
        keep_keys.start()

        def clear(g):
            scores[g] = jnp.full((1, LANES), -1.0, jnp.float32)

        each(0, groups, clear)
        keep_keys.wait()
        from_sources(lambda slot, k, device: key_copy(k, slot).wait_recv())

        def sum_keys(g):
            acc = got_keys[g * per]
            for i in range(1, per):
                acc = acc + got_keys[g * per + i]
            key_rows[0, g] = acc

        each(0, groups, sum_keys)
        key_forward.start()
        make_cols(0)
        keep_rows.wait()
        forward_copy(slot_of(my_turn)).start()

        def arrive(slot, k, device):
            rows_copy(k, slot).wait_recv()
            forward_copy(slot).start()

        def send_back(start, stop):
            from_sources(lambda slot, k, device: back_copy(slot, k, device).start(), start, stop)

        def forwarded(start, stop):
            each(start, stop, lambda slot: forward_copy(slot).wait_recv())

        if tiles == 2:
            middle = half + 1
            from_sources(arrive, 0, half)
            key_forward.wait_recv()
            make_cols(1)
            score(0, 0, 0)
            from_sources(arrive, half, middle)
            forwarded(0, blocks)
            score(1, 0, 0)
            from_sources(arrive, middle)
            score(0, 1, 0, 2)
            score(0, 0, 1)
            score(1, 1, 0)
            forwarded(blocks, sources)
            score(1, 0, 1)
            send_back(0, half)
            score(1, 1, 1)
            send_back(half, owners)
        else:
            from_sources(arrive)
            key_forward.wait_recv()
            make_cols(1)
            forwarded(0, sources)
            for j in range(2):
                each(0, tiles, lambda qt, j=j: each(0, tiles, lambda kt: score(j, qt, kt)))
            send_back(0, owners)
        keep_scores = pltpu.make_async_copy(scores.at[slot_of(my_turn) // per], got_scores.at[my_turn], own_sem.at[2])
        keep_scores.start()
        keep_scores.wait()

    to_owners(lambda k: back_copy(slot_of(k), k, owner_device(k)).wait_recv())

    def pick(k, acc):
        return jnp.where(rel_col == number(k), got_scores[k], acc)

    found = jnp.zeros((docs, LANES), jnp.float32)
    if owners <= UNROLL_UP_TO:
        for k in range(owners):
            found = pick(k, found)
    else:
        found = lax.fori_loop(0, owners, pick, found)
    result = jnp.sum(jnp.where(lanes == lane_col, found, 0.0), axis=1, keepdims=True)
    out_ref[...] = jnp.sum(jnp.where(eye, result, 0.0), axis=0, keepdims=True)

    def sent(k):
        key_copy(k, slot_of(k)).wait_send()
        rows_copy(k, slot_of(k)).wait_send()

    to_owners(sent)

    @pl.when(is_owner)
    def _():
        key_forward.wait_send()
        each(0, sources, lambda slot: forward_copy(slot).wait_send())
        from_sources(lambda slot, k, device: back_copy(slot, k, device).wait_send())


def per_device(total, embeddings, cluster_id, rank):
    owners = lax.axis_size("docs")
    pairs = lax.axis_size("split") // 2
    docs, width = embeddings.shape
    cap = 2 * docs // owners
    cap = -(-cap // ROW_TILE) * ROW_TILE
    sources = owners * pairs
    groups = sources * cap // LANES
    dma = pltpu.SemaphoreType.DMA
    out = pl.pallas_call(
        functools.partial(kernel, owners, pairs, cap, float(total)),
        out_shape=jax.ShapeDtypeStruct((1, docs), jnp.float32),
        in_specs=[pl.BlockSpec(memory_space=pl.ANY)] + [pl.BlockSpec(memory_space=pltpu.VMEM)] * 2,
        out_specs=pl.BlockSpec(memory_space=pltpu.VMEM),
        scratch_shapes=[
            pltpu.VMEM((docs, width), embeddings.dtype),
            dma,
            pltpu.VMEM((owners, cap, width), jnp.bfloat16),
            pltpu.VMEM((2, sources, cap, width), jnp.bfloat16),
            pltpu.VMEM((owners, 1, LANES), jnp.float32),
            pltpu.VMEM((sources, 1, LANES), jnp.float32),
            pltpu.VMEM((2, groups, 1, LANES), jnp.float32),
            pltpu.VMEM((2, groups, LANES, 1), jnp.float32),
            pltpu.VMEM((groups, 1, LANES), jnp.float32),
            pltpu.VMEM((owners, 1, LANES), jnp.float32),
            dma((3,)),
            dma((owners,)), dma((sources,)),
            dma((sources,)), dma((sources,)),
            dma((owners,)), dma((sources,)),
            dma, dma,
            dma((sources,)), dma((owners,)),
        ],
        compiler_params=pltpu.CompilerParams(
            collective_id=0, has_side_effects=True, vmem_limit_bytes=860 * 64 * 1024
        ),
    )(embeddings, cluster_id.reshape(1, docs), rank.reshape(1, docs))
    return out.reshape(docs)


def solution(mesh):
    placed = (P(("docs", "split"), None), P(("docs", "split")), P(("docs", "split")))

    def run(embeddings, cluster_id, rank):
        return jax.shard_map(
            functools.partial(per_device, embeddings.shape[0]),
            mesh=mesh, in_specs=placed, out_specs=P(("docs", "split")), check_vma=False,
        )(embeddings, cluster_id, rank)

    return run
```

```python
import functools

import jax
import jax.numpy as jnp
from jax import lax
from jax.experimental import pallas as pl
from jax.experimental.pallas import tpu as pltpu
from jax.sharding import PartitionSpec as P

CL_DEV = 2
EPSILON = 1e-06
LANES = 128
ROW_TILE = 16
UNROLL_UP_TO = 8
MESH = pl.DeviceIdType.MESH


def xor(a, b, size):
    out, bit = 0, 1
    while bit < size:
        out = out + bit * (((a // bit) + (b // bit)) % 2)
        bit *= 2
    return out


def each(start, stop, body):
    if stop - start <= UNROLL_UP_TO:
        for i in range(start, stop):
            body(i)
    else:
        lax.fori_loop(start, stop, lambda i, c: (body(i), c)[1], 0)


def kernel(
    owners, pairs, cap, total,
    emb_hbm, cluster_ref, rank_ref, out_ref,
    emb_ref, load_sem, send_rows, rows, send_keys, got_keys, key_rows, key_cols, scores,
    got_scores, own_sem, rows_out, rows_in, fwd_out, fwd_in, keys_out, keys_in, kfwd_out, kfwd_in, back_out, back_in,
):
    docs, width = emb_ref.shape
    per = LANES // cap
    groups = key_rows.shape[1]
    sources = owners * pairs
    me = lax.axis_index("docs")
    mine = lax.axis_index("split")
    pair, core = mine // 2, mine % 2
    first = (owners - owners // pairs) // 2
    is_owner = (me >= first) & (me < first + owners // pairs)
    my_owner = (me - first) * pairs + pair
    half = owners // 2

    def distance(i):
        return owners - 1 - i // 2 - (i % 2) * half

    def turn(d):
        near = 1 - d // half
        return 2 * (owners - 1 - near * half - d) + near

    my_turn = turn(xor(me, jnp.where(is_owner, my_owner, 0), owners))

    load = pltpu.make_async_copy(emb_hbm, emb_ref, load_sem)
    load.start()

    def owner_device(i):
        o = xor(me, distance(i), owners)
        return {"docs": first + o // pairs, "split": (o % pairs) * 2 + core}

    def not_self(i):
        return jnp.logical_not(is_owner & (my_turn == i))

    def slot_of(i):
        return i * pairs + pair

    def to_owners(body):
        def one(i):
            @pl.when(not_self(i))
            def _():
                body(i)

        each(0, owners, one)

    def from_sources(body, start=0, stop=owners):
        def one(i):
            p = xor(my_owner, distance(i), owners)
            for x in range(pairs):
                @pl.when(jnp.logical_not((p == me) & (pair == x)))
                def _():
                    body(i * pairs + x, i, {"docs": p, "split": x * 2 + core})

        each(start, stop, one)

    sibling = {"split": pair * 2 + (1 - core)}
    barrier = pltpu.get_barrier_semaphore()

    def greet(device):
        pl.semaphore_signal(barrier, inc=1, device_id=device, device_id_type=MESH)

    to_owners(lambda k: greet(owner_device(k)))

    @pl.when(is_owner)
    def _():
        greet(sibling)
        from_sources(lambda slot, k, device: greet(device))

    def copy(src, dst, out_sem, in_sem, device):
        return pltpu.make_async_remote_copy(
            src_ref=src, dst_ref=dst, send_sem=out_sem, recv_sem=in_sem, device_id=device, device_id_type=MESH
        )

    def rows_copy(k, slot):
        return copy(send_rows.at[k], rows.at[0, slot], rows_out.at[k], rows_in.at[slot], owner_device(k))

    def key_copy(k, slot):
        return copy(send_keys.at[k], got_keys.at[slot], keys_out.at[k], keys_in.at[slot], owner_device(k))

    def forward_copy(slot):
        return copy(rows.at[0, slot], rows.at[1, slot], fwd_out.at[slot], fwd_in.at[slot], sibling)

    key_forward = copy(key_rows.at[0], key_rows.at[1], kfwd_out, kfwd_in, sibling)

    def back_copy(slot, k, device):
        return copy(scores.at[slot // per], got_scores.at[k], back_out.at[slot], back_in.at[k], device)

    row_id = lax.broadcasted_iota(jnp.int32, (docs, docs), 0)
    lane_id = lax.broadcasted_iota(jnp.int32, (docs, docs), 1)
    eye = row_id == lane_id

    def column(row):
        return jnp.sum(jnp.where(eye, row, 0.0), axis=1, keepdims=True)

    cluster = cluster_ref[...]
    owner = lax.shift_right_logical(cluster, CL_DEV.bit_length() - 1)
    local = cluster - owner * CL_DEV
    key = (local + 1).astype(jnp.float32) * total + rank_ref[...].astype(jnp.float32)
    apart = jnp.bitwise_xor(owner, me)
    turns = jnp.where(apart >= half, 2 * (owners - 1 - apart), 2 * (half - 1 - apart) + 1)
    rel = turns.astype(jnp.float32)
    rel_col, key_col = column(rel), column(key)
    same = rel_col == rel
    before = jnp.sum(jnp.where(same & (row_id < lane_id), 1.0, 0.0), axis=0, keepdims=True)
    before_col = jnp.sum(jnp.where(same & (lane_id < row_id), 1.0, 0.0), axis=1, keepdims=True)
    target = (rel * cap + before).astype(jnp.int32)
    lanes = lax.broadcasted_iota(jnp.int32, (docs, LANES), 1)
    lane_col = before_col.astype(jnp.int32) + jnp.bitwise_and(slot_of(rel_col.astype(jnp.int32)), per - 1) * cap
    placed = jnp.where(lanes == lane_col, key_col, 0.0)

    def number(k):
        return jnp.float32(k) if isinstance(k, int) else k.astype(jnp.float32)

    def put_keys(k):
        send_keys[k] = jnp.sum(jnp.where(rel_col == number(k), placed, 0.0), axis=0, keepdims=True)

    each(0, owners, put_keys)

    load.wait()
    values = emb_ref[...].astype(jnp.float32)
    norm = jnp.sqrt(jnp.sum(values * values, axis=1, keepdims=True) + EPSILON)
    unit = (values * (1.0 / norm)).astype(jnp.bfloat16)
    slot_id = lax.broadcasted_iota(jnp.int32, (cap, docs), 0)

    @pl.when(is_owner)
    def _():
        pl.semaphore_wait(barrier, owners - 1 + sources - 1 + 1)

    @pl.when(jnp.logical_not(is_owner))
    def _():
        pl.semaphore_wait(barrier, owners)

    to_owners(lambda i: key_copy(i, slot_of(i)).start())

    def send(i):
        pick = jnp.where(slot_id + i * cap == target, 1.0, 0.0).astype(jnp.bfloat16)
        send_rows[i] = jnp.dot(pick, unit, preferred_element_type=jnp.float32).astype(jnp.bfloat16)

        @pl.when(not_self(i))
        def _():
            rows_copy(i, slot_of(i)).start()

    @pl.when(is_owner)
    def _():
        each(0, owners, send)

    @pl.when(jnp.logical_not(is_owner))
    def _():
        def swapped(i):
            send(2 * i + 1)
            send(2 * i)

        each(0, half, swapped)

    size = min(2, groups)
    tile = size * LANES
    tiles = groups // size
    blocks = tile // cap
    square = lax.broadcasted_iota(jnp.int32, (LANES, LANES), 0) == lax.broadcasted_iota(jnp.int32, (LANES, LANES), 1)

    def make_cols(j):
        def one(g):
            key_cols[j, g] = jnp.sum(jnp.where(square, key_rows[j, g], 0.0), axis=1, keepdims=True)

        each(0, groups, one)

    def tile_rows(j, t, n=1):
        return rows[j, pl.ds(t * blocks, n * blocks)].reshape(n * tile, width)

    def score(j, qt, kt, n=1):
        q = jnp.concatenate([key_rows[0, qt * size + i] for i in range(size)], axis=1)
        base = jnp.floor(q * (1.0 / total)) * total
        c = jnp.concatenate([key_cols[j, kt * size + i] for i in range(n * size)], axis=0)
        dots = lax.dot_general(
            tile_rows(j, kt, n), tile_rows(0, qt), (((1,), (1,)), ((), ())), preferred_element_type=jnp.float32
        )
        best = jnp.max(jnp.where((c < q) & (c >= base), dots, -1.0), axis=0, keepdims=True)
        for i in range(size):
            part = best[:, i * LANES:(i + 1) * LANES]
            scores[qt * size + i] = jnp.maximum(scores[qt * size + i], part)

    @pl.when(is_owner)
    def _():
        keep_rows = pltpu.make_async_copy(send_rows.at[my_turn], rows.at[0, slot_of(my_turn)], own_sem.at[0])
        keep_keys = pltpu.make_async_copy(send_keys.at[my_turn], got_keys.at[slot_of(my_turn)], own_sem.at[1])
        keep_rows.start()
        keep_keys.start()

        def clear(g):
            scores[g] = jnp.full((1, LANES), -1.0, jnp.float32)

        each(0, groups, clear)
        keep_keys.wait()
        from_sources(lambda slot, k, device: key_copy(k, slot).wait_recv())

        def sum_keys(g):
            acc = got_keys[g * per]
            for i in range(1, per):
                acc = acc + got_keys[g * per + i]
            key_rows[0, g] = acc

        each(0, groups, sum_keys)
        key_forward.start()
        make_cols(0)
        keep_rows.wait()
        forward_copy(slot_of(my_turn)).start()

        def arrive(slot, k, device):
            rows_copy(k, slot).wait_recv()
            forward_copy(slot).start()

        def forwarded(start, stop):
            each(start, stop, lambda slot: forward_copy(slot).wait_recv())

        if tiles == 2:
            middle = half + 1
            from_sources(arrive, 0, half)
            key_forward.wait_recv()
            make_cols(1)
            score(0, 0, 0)
            from_sources(arrive, half, middle)
            forwarded(0, blocks)
            score(1, 0, 0)
            from_sources(arrive, middle)
            score(0, 1, 0, 2)
            score(0, 0, 1)
            score(1, 1, 0)
            forwarded(blocks, sources)
            score(1, 1, 1)
            score(1, 0, 1)
        else:
            from_sources(arrive)
            key_forward.wait_recv()
            make_cols(1)
            forwarded(0, sources)
            for j in range(2):
                each(0, tiles, lambda qt, j=j: each(0, tiles, lambda kt: score(j, qt, kt)))
        keep_scores = pltpu.make_async_copy(scores.at[slot_of(my_turn) // per], got_scores.at[my_turn], own_sem.at[2])
        keep_scores.start()
        from_sources(lambda slot, k, device: back_copy(slot, k, device).start())
        keep_scores.wait()

    to_owners(lambda k: back_copy(slot_of(k), k, owner_device(k)).wait_recv())

    def pick(k, acc):
        return jnp.where(rel_col == number(k), got_scores[k], acc)

    found = jnp.zeros((docs, LANES), jnp.float32)
    if owners <= UNROLL_UP_TO:
        for k in range(owners):
            found = pick(k, found)
    else:
        found = lax.fori_loop(0, owners, pick, found)
    result = jnp.sum(jnp.where(lanes == lane_col, found, 0.0), axis=1, keepdims=True)
    out_ref[...] = jnp.sum(jnp.where(eye, result, 0.0), axis=0, keepdims=True)

    def sent(k):
        key_copy(k, slot_of(k)).wait_send()
        rows_copy(k, slot_of(k)).wait_send()

    to_owners(sent)

    @pl.when(is_owner)
    def _():
        key_forward.wait_send()
        each(0, sources, lambda slot: forward_copy(slot).wait_send())
        from_sources(lambda slot, k, device: back_copy(slot, k, device).wait_send())


def per_device(total, embeddings, cluster_id, rank):
    owners = lax.axis_size("docs")
    pairs = lax.axis_size("split") // 2
    docs, width = embeddings.shape
    cap = 2 * docs // owners
    cap = -(-cap // ROW_TILE) * ROW_TILE
    sources = owners * pairs
    groups = sources * cap // LANES
    dma = pltpu.SemaphoreType.DMA
    out = pl.pallas_call(
        functools.partial(kernel, owners, pairs, cap, float(total)),
        out_shape=jax.ShapeDtypeStruct((1, docs), jnp.float32),
        in_specs=[pl.BlockSpec(memory_space=pl.ANY)] + [pl.BlockSpec(memory_space=pltpu.VMEM)] * 2,
        out_specs=pl.BlockSpec(memory_space=pltpu.VMEM),
        scratch_shapes=[
            pltpu.VMEM((docs, width), embeddings.dtype),
            dma,
            pltpu.VMEM((owners, cap, width), jnp.bfloat16),
            pltpu.VMEM((2, sources, cap, width), jnp.bfloat16),
            pltpu.VMEM((owners, 1, LANES), jnp.float32),
            pltpu.VMEM((sources, 1, LANES), jnp.float32),
            pltpu.VMEM((2, groups, 1, LANES), jnp.float32),
            pltpu.VMEM((2, groups, LANES, 1), jnp.float32),
            pltpu.VMEM((groups, 1, LANES), jnp.float32),
            pltpu.VMEM((owners, 1, LANES), jnp.float32),
            dma((3,)),
            dma((owners,)), dma((sources,)),
            dma((sources,)), dma((sources,)),
            dma((owners,)), dma((sources,)),
            dma, dma,
            dma((sources,)), dma((owners,)),
        ],
        compiler_params=pltpu.CompilerParams(
            collective_id=0, has_side_effects=True, vmem_limit_bytes=860 * 64 * 1024
        ),
    )(embeddings, cluster_id.reshape(1, docs), rank.reshape(1, docs))
    return out.reshape(docs)


def solution(mesh):
    placed = (P(("docs", "split"), None), P(("docs", "split")), P(("docs", "split")))

    def run(embeddings, cluster_id, rank):
        return jax.shard_map(
            functools.partial(per_device, embeddings.shape[0]),
            mesh=mesh, in_specs=placed, out_specs=P(("docs", "split")), check_vma=False,
        )(embeddings, cluster_id, rank)

    return run
```
